128 devices in a mesh: gx: 8 (over z, y_lo), gy: 16 (over y_hi, x, core).
Axes of the slice: x: 4, y: 4 (y_hi: 2, y_lo: 2; y = y_hi * 2 + y_lo), z: 4, core: 2. Of those that a mesh axis runs over, the one named last changes fastest.
Arguments:
- layer_input: bfloat16 [128, 128, 20, 1024], P('gx', 'gy'), may hold values from -6 to 6
- cotangent: bfloat16 [128, 128, 20, 1024], P('gx', 'gy'), may hold values from -6 to 6
- spectral_weight: bfloat16 [32, 32, 20, 20, 2, 256], P('gx', 'gy'), may hold values from -1.1953125 to 1.1953125
- mixer_weight: bfloat16 [20, 20], replicated, may hold values from -1.25 to 1.25
- bias_vector: float32 [20], replicated, may hold values from -3 to 3
Outputs:
- input_grad: bfloat16 [128, 128, 20, 1024], P('gx', 'gy')
- spectral_grad: float32 [32, 32, 20, 20, 2, 256], P('gx', 'gy')
- mixer_grad: float32 [20, 20], replicated
- bias_grad: float32 [20], replicated
The draws below stay inside these ranges and needn't reach their ends.
All inputs are finite; a program needn't handle non-finite values.
Results may differ from the reference program's by a relative error of at most 0.038.
Values may be sent and summed in bfloat16 or wider, within the bound.
A program may use at most 192 MiB of HBM per device.

```python
import math
import jax
import jax.numpy as jnp
from jax import lax

NX = 128
NY = 128
NZ = 64
NT = 16
C = 20
MZ = 16
MT = 8
KX = 32
KY = 32
KZT = 256
NZT = 1024


def block_levels(stream_key, shape, cuts, low, high):
    def one(position, blocks):
        heights = jax.random.uniform(jax.random.fold_in(jax.random.fold_in(stream_key, 6), position), (blocks,), jnp.float32, low / len(cuts), high / len(cuts))
        return jnp.repeat(jnp.exp(heights), shape[position] // blocks).reshape((-1,) + (1,) * (len(shape) - position - 1))

    gain = one(*cuts[0])
    for cut in cuts[1:]:
        gain = gain * one(*cut)
    return gain


def bell_draw(own_key, extent, width, reach, pieces=(), held_as=jnp.bfloat16):
    gain = block_levels(own_key, extent, pieces, -0.22, 0.18) if pieces else 1.0
    values = jax.random.normal(own_key, extent, jnp.float32) * width * gain
    return jnp.minimum(jnp.maximum(values, -reach), reach).astype(held_as)


def setup_inputs(seed: int = 0) -> dict:
    key_of = jax.random.split(jax.random.key(seed), 6)
    layer_input = bell_draw(key_of[0], (NX, NY, C, NZT), 1.0, 6.0, ((0, 8), (1, 16)))
    cotangent = bell_draw(key_of[1], (NX, NY, C, NZT), 1.0, 6.0, ((0, 8), (1, 16)))
    spectral_weight = bell_draw(key_of[2], (KX, KY, C, C, 2, KZT), 0.2, 1.1953125, ((0, 8), (1, 16)))
    mixer_weight = bell_draw(key_of[3], (C, C), C ** -0.5, 1.25)
    bias_vector = bell_draw(key_of[4], (C,), 0.5, 3.0, (), jnp.float32)
    return {"layer_input": layer_input, "cotangent": cotangent, "spectral_weight": spectral_weight, "mixer_weight": mixer_weight, "bias_vector": bias_vector}


def signed_frequency(number):
    values = jnp.arange(number, dtype=jnp.int32)
    return jnp.where(values < number // 2, values, values - number)

def pair_table(frequency, length):
    places = jnp.arange(length, dtype=jnp.int32)
    phases = jnp.mod(frequency[:, None] * places[None, :], length).astype(jnp.float32)
    angles = phases * (-2.0 * math.pi / length)
    factor = float(length) ** (-0.5)
    cosine = jnp.cos(angles) * factor
    sine_part = jnp.sin(angles) * factor
    top_rows = jnp.stack([cosine, -sine_part], -1)
    low_rows = jnp.stack([sine_part, cosine], -1)
    return jnp.stack([top_rows, low_rows], 1).astype(jnp.bfloat16)

def depth_table():
    depth_freq = signed_frequency(2 * MZ)
    time_freq = jnp.arange(MT, dtype=jnp.int32)
    depth_pos = jnp.arange(NZ, dtype=jnp.int32)
    time_pos = jnp.arange(NT, dtype=jnp.int32)
    cell_count = NZ * NT
    phases = depth_pos[:, None, None, None] * depth_freq[None, None, :, None] * NT + time_pos[None, :, None, None] * time_freq[None, None, None, :] * NZ
    phases = jnp.mod(phases, cell_count).astype(jnp.float32).reshape(cell_count, 2 * MZ * MT)
    angles = phases * (-2.0 * math.pi / cell_count)
    factor = float(cell_count) ** (-0.5)
    stacked = jnp.stack([jnp.cos(angles) * factor, jnp.sin(angles) * factor], 1)
    return stacked.reshape(cell_count, 4 * MZ * MT).astype(jnp.bfloat16)

def mode_weight():
    orders = jnp.arange(2 * MZ * MT, dtype=jnp.int32) % MT
    return jnp.where(orders == 0, 1.0, 2.0).astype(jnp.float32)

def gelu_slope(values):
    normal_cdf = 0.5 * (1.0 + jax.scipy.special.erf(values * (1.0 / math.sqrt(2.0))))
    density = jnp.exp(-0.5 * values * values) * (1.0 / math.sqrt(2.0 * math.pi))
    return normal_cdf + values * density

def reference(layer_input, cotangent, spectral_weight, mixer_weight, bias_vector):
    highest = lax.Precision.HIGHEST
    x_table = pair_table(signed_frequency(KX), NX).astype(jnp.float32)
    y_table = pair_table(signed_frequency(KY), NY).astype(jnp.float32)
    depth_matrix = depth_table().astype(jnp.float32)
    weights_mode = mode_weight()
    mixer = mixer_weight.astype(jnp.float32)

    def spectral_forward(grid):

        def slab_modes(grid_slab):
            flattened = grid_slab.astype(jnp.float32).reshape(-1, NZT)
            product = jnp.dot(flattened, depth_matrix, precision=highest)
            return product.astype(jnp.bfloat16).reshape(NY, C, 2, KZT)
        depth_modes = lax.map(slab_modes, grid)
        y_modes = jnp.einsum('lpyq,xycqk->xlcpk', y_table, depth_modes.astype(jnp.float32), precision=highest).astype(jnp.bfloat16)
        return jnp.einsum('apxq,xlcqk->alcpk', x_table, y_modes.astype(jnp.float32), precision=highest).astype(jnp.bfloat16)

    def spectral_inverse(spectrum):
        inverse_x = jnp.einsum('aqxp,alcqk->xlcpk', x_table, spectrum.astype(jnp.float32), precision=highest).astype(jnp.bfloat16)
        return jnp.einsum('lqyp,xlcqk->xycpk', y_table, inverse_x.astype(jnp.float32), precision=highest).astype(jnp.bfloat16)

    def back_depth(spec_slab):
        flattened = spec_slab.astype(jnp.float32).reshape(-1, 2 * KZT)
        return jnp.dot(flattened, depth_matrix.T, precision=highest).reshape(NY, C, NZT)
    spectral_modes = spectral_forward(layer_input)
    weight_all = spectral_weight.astype(jnp.float32)
    weight_real = weight_all[:, :, :, :, 0]
    weight_imag = weight_all[:, :, :, :, 1]
    mode_real = spectral_modes[:, :, :, 0].astype(jnp.float32)
    mode_imag = spectral_modes[:, :, :, 1].astype(jnp.float32)

    def contract(weights, values):
        return jnp.einsum('abiok,abik->abok', weights, values, precision=highest)

    def adjoint(weights, values):
        return jnp.einsum('abiok,abok->abik', weights, values, precision=highest)
    real_sum = contract(weight_real, mode_real) - contract(weight_imag, mode_imag)
    imag_sum = contract(weight_real, mode_imag) + contract(weight_imag, mode_real)
    spectrum = (jnp.stack([real_sum, imag_sum], 3) * weights_mode).astype(jnp.bfloat16)
    grid_spectrum = spectral_inverse(spectrum)

    def forward_slab(operands):
        spec_slab, input_slab, cot_slab = operands
        pointwise = jnp.einsum('yik,io->yok', input_slab.astype(jnp.float32), mixer, precision=highest)
        pre_act = back_depth(spec_slab) + pointwise + bias_vector[None, :, None]
        return (cot_slab.astype(jnp.float32) * gelu_slope(pre_act)).astype(jnp.bfloat16)
    pre_grad = lax.map(forward_slab, (grid_spectrum, layer_input, cotangent))
    grad_modes = spectral_forward(pre_grad)
    scaled = grad_modes.astype(jnp.float32) * weights_mode
    scaled_real = scaled[:, :, :, 0]
    scaled_imag = scaled[:, :, :, 1]
    grad_real = mode_real[:, :, :, None] * scaled_real[:, :, None] + mode_imag[:, :, :, None] * scaled_imag[:, :, None]
    grad_imag = mode_real[:, :, :, None] * scaled_imag[:, :, None] - mode_imag[:, :, :, None] * scaled_real[:, :, None]
    spectral_grad = jnp.stack([grad_real, grad_imag], 4)
    back_real = adjoint(weight_real, scaled_real) + adjoint(weight_imag, scaled_imag)
    back_imag = adjoint(weight_real, scaled_imag) - adjoint(weight_imag, scaled_real)
    grad_spectrum = jnp.stack([back_real, back_imag], 3).astype(jnp.bfloat16)
    grid_back = spectral_inverse(grad_spectrum)

    def backward_slab(operands):
        spec_slab, grad_slab, input_slab = operands
        grad_f = grad_slab.astype(jnp.float32)
        pointwise = jnp.einsum('yok,io->yik', grad_f, mixer, precision=highest)
        result = (back_depth(spec_slab) + pointwise).astype(jnp.bfloat16)
        mixer_part = jnp.einsum('yik,yok->io', input_slab.astype(jnp.float32), grad_f, precision=highest)
        bias_part = lax.optimization_barrier(jnp.sum(grad_f, axis=(0, 2)))
        return (result, mixer_part, bias_part)
    input_grad, mixer_parts, bias_parts = lax.map(backward_slab, (grid_back, pre_grad, layer_input))
    scale_factor = 1.0 / math.sqrt(NX * NY * NZT)
    return (input_grad, spectral_grad, lax.optimization_barrier(jnp.sum(mixer_parts, 0)) * scale_factor, lax.optimization_barrier(jnp.sum(bias_parts, 0)) * scale_factor)
```

```python
import functools
import math

import jax
import jax.numpy as jnp
import ml_dtypes
import numpy as np
from jax import lax
from jax.experimental import pallas as pl
from jax.experimental.pallas import tpu as pltpu
from jax.sharding import PartitionSpec as P

NX = 128
NY = 128
NZ = 64
NT = 16
C = 20
MZ = 16
MT = 8
KX = 32
KY = 32
KZT = 256
NZT = 1024
GX = 8
GY = 16
HALF = 8
XL = NX // GX
YL = NY // GY
CHUNKS = 5
CC = C // CHUNKS
ROWS = C * YL
CR = CC * YL
BF = jnp.bfloat16
F32 = jnp.float32
MESH = pl.DeviceIdType.MESH


def signed_frequency(number):
    values = np.arange(number)
    return np.where(values < number // 2, values, values - number)


def pair_table(frequency, length):
    places = np.arange(length)
    phases = np.mod(frequency[:, None] * places[None, :], length)
    angles = phases * (-2.0 * math.pi / length)
    factor = float(length) ** (-0.5)
    cosine = np.cos(angles) * factor
    sine_part = np.sin(angles) * factor
    top_rows = np.stack([cosine, -sine_part], -1)
    low_rows = np.stack([sine_part, cosine], -1)
    return np.stack([top_rows, low_rows], 1)


def depth_table():
    fz = signed_frequency(2 * MZ)
    ft = np.arange(MT)
    z = np.arange(NZ)
    t = np.arange(NT)
    phases = (
        z[:, None, None, None] * fz[None, None, :, None] * NT
        + t[None, :, None, None] * ft[None, None, None, :] * NZ
    )
    phases = np.mod(phases, NZT).reshape(NZT, KZT)
    angles = phases * (-2.0 * math.pi / NZT)
    factor = float(NZT) ** (-0.5)
    stacked = np.stack([np.cos(angles) * factor, np.sin(angles) * factor], 1)
    return stacked.reshape(NZT, 2 * KZT)


def as_bf16(table):
    return np.ascontiguousarray(table).astype(np.float32).astype(ml_dtypes.bfloat16)


@functools.lru_cache(maxsize=None)
def tables():
    depth = depth_table()
    xt = pair_table(signed_frequency(KX), NX)
    yt = pair_table(signed_frequency(KY), NY)
    eye_c = np.eye(CC)
    eye_l = np.eye(2)
    yv = yt.reshape(GY, 2, 2, 2, HALF, YL, 2)
    yf = np.einsum("jlphsyq,cd->hjcplsdqy", yv, eye_c).reshape(2, 256, 512)
    xv = xt.reshape(GX, 4, 2, GX, HALF, 2, 2)
    xf = np.einsum("iapgsxq,cd,lm->giacplsxdqm", xv, eye_c, eye_l).reshape(GX, 512, 256)
    xi = np.transpose(xf, (0, 2, 1))
    xf = np.concatenate([xf, xf], 2)
    yi = np.transpose(yf, (0, 2, 1))
    return tuple(as_bf16(v) for v in (depth, depth.T, yf, yi, xf, xi))


def mode_weight():
    orders = jnp.arange(KZT, dtype=jnp.int32) % MT
    return jnp.where(orders == 0, 1.0, 2.0).astype(F32)


def gelu_slope(values):
    normal_cdf = 0.5 * (1.0 + lax.erf(values * (1.0 / math.sqrt(2.0))))
    density = jnp.exp(-0.5 * values * values) * (1.0 / math.sqrt(2.0 * math.pi))
    return normal_cdf + values * density


def mm(a, b):
    return jnp.dot(a, b, preferred_element_type=F32)


class Place:
    def __init__(self):
        self.gx = lax.axis_index("gx")
        self.gy = lax.axis_index("gy")
        self.lo = lax.rem(self.gy, HALF)
        self.hi = lax.div(self.gy, HALF)

    def x_peer(self, d):
        return lax.rem(self.gx + d, GX)

    def y_peer(self, d):
        return lax.rem(self.gy + d, GY)

    def half_peer(self, d):
        return lax.rem(self.lo + d, HALF)

    def greet(self):
        barrier = pltpu.get_barrier_semaphore()
        for d in range(1, GX):
            pl.semaphore_signal(
                barrier, inc=1, device_id={"gx": self.x_peer(d)}, device_id_type=MESH
            )
        for d in range(1, GY):
            pl.semaphore_signal(
                barrier, inc=1, device_id={"gy": self.y_peer(d)}, device_id_type=MESH
            )
        pl.semaphore_wait(barrier, GX + GY - 2)


def remote(src, dst, send, recv, device):
    pltpu.make_async_remote_copy(
        src_ref=src, dst_ref=dst, send_sem=send, recv_sem=recv,
        device_id=device, device_id_type=MESH,
    ).start()


def local(src, dst, sem):
    pltpu.make_async_copy(src, dst, sem).start()


def wait_for(region, sem):
    pltpu.make_async_copy(region, region, sem).wait()


def half_exchange(me, src, dst, send, recv):
    for d in range(1, HALF):
        peer = me.half_peer(d)
        remote(src.at[peer], dst.at[me.lo], send, recv, {"gy": me.hi * HALF + peer})
    local(src.at[me.lo], dst.at[me.lo], recv)


def row_exchange(me, src, dst, send, recv):
    for d in range(1, GY):
        peer = me.y_peer(d)
        remote(src.at[peer], dst.at[me.gy], send, recv, {"gy": peer})
    local(src.at[me.gy], dst.at[me.gy], recv)


def row_spread(me, src, dst, send, recv):
    for d in range(1, GY):
        peer = me.y_peer(d)
        remote(src.at[lax.rem(peer, HALF)], dst.at[me.gy], send, recv, {"gy": peer})
    local(src.at[me.lo], dst.at[me.gy], recv)


def column_exchange(me, src, dst, send, recv):
    for d in range(1, GX):
        peer = me.x_peer(d)
        remote(src.at[peer], dst.at[me.gx], send, recv, {"gx": peer})
    local(src.at[me.gx], dst.at[me.gx], recv)


def column_spread(me, src, dst, send, recv):
    for d in range(1, GX):
        remote(src, dst.at[me.gx], send, recv, {"gx": me.x_peer(d)})
    local(src, dst.at[me.gx], recv)


FORWARD_SCRATCH = [
    pltpu.VMEM((CHUNKS, HALF, 128, KZT), BF),
    pltpu.VMEM((CHUNKS, HALF, 128, KZT), BF),
    pltpu.VMEM((CHUNKS, GY, 32, KZT), BF),
    pltpu.VMEM((CHUNKS, GY, 32, KZT), BF),
    pltpu.VMEM((CHUNKS, GX, 64, KZT), BF),
    pltpu.VMEM((CHUNKS, GX, 64, KZT), BF),
    pltpu.SemaphoreType.DMA((3, CHUNKS)),
    pltpu.SemaphoreType.DMA((3, CHUNKS)),
]
INVERSE_SCRATCH = [
    pltpu.VMEM((CHUNKS, GX, 64, KZT), BF),
    pltpu.VMEM((CHUNKS, HALF, 32, KZT), BF),
    pltpu.VMEM((CHUNKS, GY, 32, KZT), BF),
    pltpu.VMEM((CHUNKS, HALF, 128, KZT), BF),
    pltpu.VMEM((CHUNKS, HALF, 128, KZT), BF),
    pltpu.SemaphoreType.DMA((3, CHUNKS)),
    pltpu.SemaphoreType.DMA((3, CHUNKS)),
]


class Forward:
    def __init__(self, me, depth, yf, xf, out, sa, ra, sb, rb, sc, rc, send, recv):
        self.me, self.depth, self.yf, self.xf, self.out = me, depth, yf, xf, out
        self.sa, self.ra, self.sb, self.rb, self.sc, self.rc = sa, ra, sb, rb, sc, rc
        self.send, self.recv = send, recv

    def put(self, c, part, parts, grid):
        count = XL // parts
        modes = mm(grid, self.depth[...])
        real = modes[:, :KZT].reshape(count, CC, 1, YL, KZT)
        imag = modes[:, KZT:].reshape(count, CC, 1, YL, KZT)
        both = jnp.concatenate([real, imag], 2).reshape(count * 64, KZT).astype(BF)
        self.sa[c, pl.ds(part * (count // 2), count // 2)] = both.reshape(count // 2, 128, KZT)

    def send_a(self, c):
        half_exchange(
            self.me, self.sa.at[c], self.ra.at[c], self.send.at[0, c], self.recv.at[0, c]
        )

    def stage_b(self, c):
        wait_for(self.ra.at[c], self.recv.at[0, c])
        for x2 in range(2):
            block = self.ra[c, :, x2 * 64 : x2 * 64 + 64, :].reshape(512, KZT)
            self.sb[c, :, x2 * 16 : x2 * 16 + 16, :] = (
                mm(self.yf[...], block).astype(BF).reshape(GY, 16, KZT)
            )
        row_exchange(
            self.me, self.sb.at[c], self.rb.at[c], self.send.at[1, c], self.recv.at[1, c]
        )

    def stage_c(self, c):
        wait_for(self.rb.at[c], self.recv.at[1, c])
        block = self.rb[c].reshape(512, KZT)
        self.sc[c] = mm(self.xf[...], block).astype(BF).reshape(GX, 64, KZT)
        column_exchange(
            self.me, self.sc.at[c], self.rc.at[c], self.send.at[2, c], self.recv.at[2, c]
        )

    def stage_d(self, c):
        wait_for(self.rc.at[c], self.recv.at[2, c])
        total = self.rc[c, 0].astype(F32)
        for source in range(1, GX):
            total = total + self.rc[c, source].astype(F32)
        self.out[c] = total.astype(BF)

    def finish(self):
        @pl.loop(0, CHUNKS)
        def _(c):
            wait_for(self.sa.at[c, pl.ds(0, HALF - 1)], self.send.at[0, c])
            wait_for(self.sb.at[c, pl.ds(0, GY - 1)], self.send.at[1, c])
            wait_for(self.sc.at[c, pl.ds(0, GX - 1)], self.send.at[2, c])


class Inverse:
    def __init__(self, me, back, yi, xi, spec, rp, sq, rq, sr, rr, send, recv):
        self.me, self.back, self.yi, self.xi, self.spec = me, back, yi, xi, spec
        self.rp, self.sq, self.rq, self.sr, self.rr = rp, sq, rq, sr, rr
        self.send, self.recv = send, recv

    def stage_p(self, c):
        column_spread(
            self.me, self.spec.at[c], self.rp.at[c], self.send.at[0, c], self.recv.at[0, c]
        )

    def stage_q(self, c):
        wait_for(self.rp.at[c], self.recv.at[0, c])
        block = self.rp[c].reshape(512, KZT)
        self.sq[c] = mm(self.xi[...], block).astype(BF).reshape(HALF, 32, KZT)
        row_spread(
            self.me, self.sq.at[c], self.rq.at[c], self.send.at[1, c], self.recv.at[1, c]
        )

    def stage_r(self, c):
        wait_for(self.rq.at[c], self.recv.at[1, c])
        for x2 in range(2):
            block = self.rq[c, :, x2 * 16 : x2 * 16 + 16, :].reshape(256, KZT)
            self.sr[c, :, x2 * 64 : x2 * 64 + 64, :] = (
                mm(self.yi[...], block).astype(BF).reshape(HALF, 64, KZT)
            )
        half_exchange(
            self.me, self.sr.at[c], self.rr.at[c], self.send.at[2, c], self.recv.at[2, c]
        )

    def ready(self, c):
        wait_for(self.rr.at[c], self.recv.at[2, c])

    def branch(self, c, part, parts):
        count = XL // parts
        block = self.rr[c, pl.ds(part * (count // 2), count // 2)].astype(F32)
        block = block.reshape(count, CC, 2, YL, KZT)
        real = block[:, :, 0].reshape(count * CR, KZT).astype(BF)
        imag = block[:, :, 1].reshape(count * CR, KZT).astype(BF)
        return mm(real, self.back[:KZT, :]) + mm(imag, self.back[KZT:, :])

    def finish(self):
        @pl.loop(0, CHUNKS)
        def _(c):
            wait_for(self.rp.at[c, pl.ds(0, GX - 1)], self.send.at[0, c])
            wait_for(self.rq.at[c, pl.ds(0, GY - 1)], self.send.at[1, c])
            wait_for(self.sr.at[c, pl.ds(0, HALF - 1)], self.send.at[2, c])


def staged(stages):
    depth = len(stages)

    @pl.loop(0, CHUNKS + depth - 1)
    def _(t):
        for s, stage in enumerate(stages):
            @pl.when(jnp.logical_and(t >= s, t < CHUNKS + s))
            def _(stage=stage, s=s):
                stage(t - s)


def first_kernel(x_hbm, depth, yf, xf, out, xbuf, xsem, *scratch):
    me = Place()

    @pl.loop(0, CHUNKS)
    def _(c):
        local(x_hbm.at[:, pl.ds(c * CR, CR), :], xbuf.at[c], xsem.at[c])

    me.greet()
    fwd = Forward(me, depth, yf, xf, out, *scratch)

    def stage_a(c):
        wait_for(xbuf.at[c], xsem.at[c])
        for part in range(2):
            fwd.put(c, part, 2, xbuf[c, part * 8 : part * 8 + 8].reshape(8 * CR, NZT))
        fwd.send_a(c)

    staged([stage_a, fwd.stage_b, fwd.stage_c, fwd.stage_d])
    fwd.finish()


def second_kernel(
    x_hbm, cot_hbm, spec, mixer, bias, depth, back, yf, yi, xf, xi, grad_hbm, out,
    xbuf, cbuf, gbuf, point, xsem, csem, gsem, *scratch
):
    me = Place()
    local(x_hbm, xbuf, xsem)

    @pl.loop(0, CHUNKS)
    def _(c):
        local(cot_hbm.at[:, pl.ds(c * CR, CR), :], cbuf.at[c], csem.at[c])

    me.greet()
    n_inverse = len(INVERSE_SCRATCH)
    inv = Inverse(me, back, yi, xi, spec, *scratch[:n_inverse])
    fwd = Forward(me, depth, yf, xf, out, *scratch[n_inverse:])

    @pl.loop(0, CHUNKS)
    def _(c):
        inv.stage_p(c)

    wait_for(xbuf, xsem)

    @pl.loop(0, XL)
    def _(x):
        point[x] = mm(mixer[...], xbuf[x]) + bias[...]

    def stage_s(c):
        inv.ready(c)
        wait_for(cbuf.at[c], csem.at[c])

        @pl.loop(0, 2)
        def _(part):
            rows = pl.ds(part * 8, 8)
            pre = inv.branch(c, part, 2)
            pre = pre + point[rows, pl.ds(c * CR, CR), :].reshape(8 * CR, NZT)
            cot = cbuf[c, rows].reshape(8 * CR, NZT).astype(F32)
            grad = (cot * gelu_slope(pre)).astype(BF)
            gbuf[c, rows] = grad.reshape(8, CR, NZT)
            fwd.put(c, part, 2, grad)

        local(gbuf.at[c], grad_hbm.at[:, pl.ds(c * CR, CR), :], gsem.at[c])
        fwd.send_a(c)

    staged([inv.stage_q, inv.stage_r, stage_s, fwd.stage_b, fwd.stage_c, fwd.stage_d])

    @pl.loop(0, CHUNKS)
    def _(c):
        wait_for(gbuf.at[c], gsem.at[c])

    inv.finish()
    fwd.finish()


def third_kernel(
    x_hbm, grad_hbm, spec, mixer, fold, back, yi, xi, out_hbm, small_out,
    xbuf, gbuf, obuf, point, mixed, one, col, two, row, xsem, gsem, osem, small, *scratch
):
    me = Place()
    local(x_hbm, xbuf, xsem)
    local(grad_hbm, gbuf, gsem)
    me.greet()
    inv = Inverse(me, back, yi, xi, spec, *scratch)

    @pl.loop(0, CHUNKS)
    def _(c):
        inv.stage_p(c)

    wait_for(xbuf, xsem)
    wait_for(gbuf, gsem)
    mixed[...] = jnp.zeros_like(mixed)

    @pl.loop(0, XL)
    def _(x):
        grad = gbuf[x]
        point[x] = mm(mixer[...], grad)
        contract = (((1,), (1,)), ((), ()))
        mixed[:ROWS, :] += lax.dot_general(xbuf[x], grad, contract, preferred_element_type=F32)
        mixed[ROWS:, :] += lax.dot_general(
            jnp.ones((8, NZT), BF), grad, contract, preferred_element_type=F32
        )

    places = mixed[:ROWS, :].shape
    same = lax.rem(lax.broadcasted_iota(jnp.int32, places, 0), YL) == lax.rem(
        lax.broadcasted_iota(jnp.int32, places, 1), YL
    )
    kept = jnp.where(same, mixed[:ROWS, :], 0.0).reshape(C, YL, ROWS).sum(1)
    stacked = jnp.concatenate([kept, mixed[ROWS : ROWS + 4, :]], 0)
    one[...] = lax.dot_general(
        stacked, fold[...], (((1,), (0,)), ((), ())),
        precision=lax.Precision.HIGHEST, preferred_element_type=F32,
    )
    for d in range(1, GX):
        remote(one, col.at[me.gx], small.at[0], small.at[1], {"gx": me.x_peer(d)})
    local(one, col.at[me.gx], small.at[1])

    def stage_s(c):
        inv.ready(c)

        @pl.loop(0, 2)
        def _(part):
            rows = pl.ds(part * 8, 8)
            total = inv.branch(c, part, 2)
            total = total + point[rows, pl.ds(c * CR, CR), :].reshape(8 * CR, NZT)
            obuf[c, rows] = total.astype(BF).reshape(8, CR, NZT)

        local(obuf.at[c], out_hbm.at[:, pl.ds(c * CR, CR), :], osem.at[c])

    staged([inv.stage_q, inv.stage_r, stage_s])

    wait_for(col, small.at[1])
    total = col[0]
    for source in range(1, GX):
        total = total + col[source]
    two[...] = total
    for d in range(1, GY):
        remote(two, row.at[me.gy], small.at[2], small.at[3], {"gy": me.y_peer(d)})
    local(two, row.at[me.gy], small.at[3])
    wait_for(row, small.at[3])
    total = row[0]
    for source in range(1, GY):
        total = total + row[source]
    small_out[...] = total
    wait_for(col.at[pl.ds(0, GX - 1)], small.at[0])
    wait_for(row.at[pl.ds(0, GY - 1)], small.at[2])

    @pl.loop(0, CHUNKS)
    def _(c):
        wait_for(obuf.at[c], osem.at[c])

    inv.finish()


ANY = pl.BlockSpec(memory_space=pl.ANY)
VM = pl.BlockSpec(memory_space=pltpu.VMEM)


def params(number):
    return pltpu.CompilerParams(
        collective_id=number, has_side_effects=True, vmem_limit_bytes=60 * 2**20
    )


def body(layer_input, cotangent, spectral_weight, mixer_weight, bias_vector):
    depth, back, yf_all, yi_all, xf_all, xi_all = (jnp.asarray(v) for v in tables())
    gx = lax.axis_index("gx")
    half = lax.axis_index("gy") // HALF
    yf = lax.dynamic_index_in_dim(yf_all, half, 0, False)
    yi = lax.dynamic_index_in_dim(yi_all, half, 0, False)
    xf = lax.dynamic_index_in_dim(xf_all, gx, 0, False)
    xi = lax.dynamic_index_in_dim(xi_all, gx, 0, False)
    weights_mode = mode_weight()
    grid = jnp.swapaxes(layer_input, 1, 2).reshape(XL, ROWS, NZT)
    cot = jnp.swapaxes(cotangent, 1, 2).reshape(XL, ROWS, NZT)
    eye = jnp.eye(YL, dtype=BF)
    mixer_forward = jnp.einsum("io,yz->oyiz", mixer_weight, eye).reshape(ROWS, ROWS)
    mixer_back = jnp.einsum("io,yz->iyoz", mixer_weight, eye).reshape(ROWS, ROWS)
    bias_rows = jnp.repeat(bias_vector, YL)[:, None]
    modes_shape = jax.ShapeDtypeStruct((CHUNKS, 64, KZT), BF)

    def unpack(modes):
        return modes.reshape(CHUNKS, 4, CC, 2, 2, KZT).transpose(1, 4, 0, 2, 3, 5).reshape(
            4, 2, C, 2, KZT
        )

    def pack(modes):
        return modes.reshape(4, 2, CHUNKS, CC, 2, KZT).transpose(2, 0, 3, 4, 1, 5).reshape(
            CHUNKS, 64, KZT
        )

    modes = pl.pallas_call(
        first_kernel,
        out_shape=modes_shape,
        in_specs=[ANY, VM, VM, VM],
        out_specs=VM,
        scratch_shapes=[
            pltpu.VMEM((CHUNKS, XL, CR, NZT), BF),
            pltpu.SemaphoreType.DMA((CHUNKS,)),
        ]
        + FORWARD_SCRATCH,
        compiler_params=params(1),
        name="first",
    )(grid, depth, yf, xf)
    spectral_modes = unpack(modes)

    def contract(weights, values):
        return jnp.einsum("abiok,abik->abok", weights, values, preferred_element_type=F32)

    def adjoint(weights, values):
        return jnp.einsum("abiok,abok->abik", weights, values, preferred_element_type=F32)

    weight_real = spectral_weight[:, :, :, :, 0]
    weight_imag = spectral_weight[:, :, :, :, 1]
    mode_real = spectral_modes[:, :, :, 0]
    mode_imag = spectral_modes[:, :, :, 1]
    real_sum = contract(weight_real, mode_real) - contract(weight_imag, mode_imag)
    imag_sum = contract(weight_real, mode_imag) + contract(weight_imag, mode_real)
    spectrum = (jnp.stack([real_sum, imag_sum], 3) * weights_mode).astype(BF)

    pre_grad, grad_modes = pl.pallas_call(
        second_kernel,
        out_shape=[jax.ShapeDtypeStruct((XL, ROWS, NZT), BF), modes_shape],
        in_specs=[ANY, ANY] + [VM] * 9,
        out_specs=[ANY, VM],
        scratch_shapes=[
            pltpu.VMEM((XL, ROWS, NZT), BF),
            pltpu.VMEM((CHUNKS, XL, CR, NZT), BF),
            pltpu.VMEM((CHUNKS, XL, CR, NZT), BF),
            pltpu.VMEM((XL, ROWS, NZT), F32),
            pltpu.SemaphoreType.DMA,
            pltpu.SemaphoreType.DMA((CHUNKS,)),
            pltpu.SemaphoreType.DMA((CHUNKS,)),
        ]
        + INVERSE_SCRATCH
        + FORWARD_SCRATCH,
        compiler_params=params(2),
        name="second",
    )(grid, cot, pack(spectrum), mixer_forward, bias_rows, depth, back, yf, yi, xf, xi)

    scaled = unpack(grad_modes) * weights_mode.astype(BF)
    scaled_real = scaled[:, :, :, 0]
    scaled_imag = scaled[:, :, :, 1]
    back_real = adjoint(weight_real, scaled_real) + adjoint(weight_imag, scaled_imag)
    back_imag = adjoint(weight_real, scaled_imag) - adjoint(weight_imag, scaled_real)
    grad_spectrum = jnp.stack([back_real, back_imag], 3).astype(BF)
    real_modes = mode_real.astype(F32)
    imag_modes = mode_imag.astype(F32)
    real_scaled = scaled_real.astype(F32)
    imag_scaled = scaled_imag.astype(F32)
    grad_real = (
        real_modes[:, :, :, None] * real_scaled[:, :, None]
        + imag_modes[:, :, :, None] * imag_scaled[:, :, None]
    )
    grad_imag = (
        real_modes[:, :, :, None] * imag_scaled[:, :, None]
        - imag_modes[:, :, :, None] * real_scaled[:, :, None]
    )
    spectral_grad = jnp.stack([grad_real, grad_imag], 4)

    fold = (jnp.arange(ROWS)[:, None] // YL == jnp.arange(128)[None, :]).astype(F32)
    input_grad, small = pl.pallas_call(
        third_kernel,
        out_shape=[
            jax.ShapeDtypeStruct((XL, ROWS, NZT), BF),
            jax.ShapeDtypeStruct((24, 128), F32),
        ],
        in_specs=[ANY, ANY] + [VM] * 6,
        out_specs=[ANY, VM],
        scratch_shapes=[
            pltpu.VMEM((XL, ROWS, NZT), BF),
            pltpu.VMEM((XL, ROWS, NZT), BF),
            pltpu.VMEM((CHUNKS, XL, CR, NZT), BF),
            pltpu.VMEM((XL, ROWS, NZT), F32),
            pltpu.VMEM((ROWS + 8, ROWS), F32),
            pltpu.VMEM((24, 128), F32),
            pltpu.VMEM((GX, 24, 128), F32),
            pltpu.VMEM((24, 128), F32),
            pltpu.VMEM((GY, 24, 128), F32),
            pltpu.SemaphoreType.DMA,
            pltpu.SemaphoreType.DMA,
            pltpu.SemaphoreType.DMA((CHUNKS,)),
            pltpu.SemaphoreType.DMA((4,)),
        ]
        + INVERSE_SCRATCH,
        compiler_params=params(3),
        name="third",
    )(grid, pre_grad, pack(grad_spectrum), mixer_back, fold, back, yi, xi)
    input_grad = jnp.swapaxes(input_grad.reshape(XL, C, YL, NZT), 1, 2)
    scale_factor = 1.0 / math.sqrt(NX * NY * NZT)
    small = small * scale_factor
    return (input_grad, spectral_grad, small[:C, :C], small[C, :C])


def solution(mesh):
    return jax.shard_map(
        body,
        mesh=mesh,
        in_specs=(
            P("gx", "gy", None, None),
            P("gx", "gy", None, None),
            P("gx", "gy", None, None, None, None),
            P(),
            P(),
        ),
        out_specs=(P("gx", "gy", None, None), P("gx", "gy", None, None, None, None), P(), P()),
        check_vma=False,
    )
```

```python
import functools
import math

import jax
import jax.numpy as jnp
import ml_dtypes
import numpy as np
from jax import lax
from jax.experimental import pallas as pl
from jax.experimental.pallas import tpu as pltpu
from jax.sharding import PartitionSpec as P

NX = 128
NY = 128
NZ = 64
NT = 16
C = 20
MZ = 16
MT = 8
KX = 32
KY = 32
KZT = 256
NZT = 1024
GX = 8
GY = 16
HALF = 8
XL = NX // GX
YL = NY // GY
CHUNKS = 5
CC = C // CHUNKS
ROWS = C * YL
CR = CC * YL
BF = jnp.bfloat16
F32 = jnp.float32
MESH = pl.DeviceIdType.MESH


def signed_frequency(number):
    values = np.arange(number)
    return np.where(values < number // 2, values, values - number)


def pair_table(frequency, length):
    places = np.arange(length)
    phases = np.mod(frequency[:, None] * places[None, :], length)
    angles = phases * (-2.0 * math.pi / length)
    factor = float(length) ** (-0.5)
    cosine = np.cos(angles) * factor
    sine_part = np.sin(angles) * factor
    top_rows = np.stack([cosine, -sine_part], -1)
    low_rows = np.stack([sine_part, cosine], -1)
    return np.stack([top_rows, low_rows], 1)


def depth_table():
    fz = signed_frequency(2 * MZ)
    ft = np.arange(MT)
    z = np.arange(NZ)
    t = np.arange(NT)
    phases = (
        z[:, None, None, None] * fz[None, None, :, None] * NT
        + t[None, :, None, None] * ft[None, None, None, :] * NZ
    )
    phases = np.mod(phases, NZT).reshape(NZT, KZT)
    angles = phases * (-2.0 * math.pi / NZT)
    factor = float(NZT) ** (-0.5)
    stacked = np.stack([np.cos(angles) * factor, np.sin(angles) * factor], 1)
    return stacked.reshape(NZT, 2 * KZT)


def as_bf16(table):
    return np.ascontiguousarray(table).astype(np.float32).astype(ml_dtypes.bfloat16)


@functools.lru_cache(maxsize=None)
def tables():
    depth = depth_table()
    xt = pair_table(signed_frequency(KX), NX)
    yt = pair_table(signed_frequency(KY), NY)
    eye_c = np.eye(CC)
    eye_l = np.eye(2)
    yv = yt.reshape(GY, 2, 2, 2, HALF, YL, 2)
    yf = np.einsum("jlphsyq,cd->hjlcpsdqy", yv, eye_c).reshape(2, 256, 512)
    xv = xt.reshape(GX, 4, 2, GX, HALF, 2, 2)
    xf = np.einsum("iapgsxq,cd,lm->gialcpsxmdq", xv, eye_c, eye_l).reshape(GX, 512, 256)
    xi = np.transpose(xf, (0, 2, 1))
    yi = np.transpose(yf, (0, 2, 1))
    return tuple(as_bf16(v) for v in (depth, depth.T, yf, yi, xf, xi))


def mode_weight(shape):
    lanes = lax.broadcasted_iota(jnp.int32, shape, len(shape) - 1)
    return jnp.where(lax.rem(lanes, MT) == 0, 1.0, 2.0).astype(F32)


def gelu_slope(values):
    normal_cdf = 0.5 * (1.0 + lax.erf(values * (1.0 / math.sqrt(2.0))))
    density = jnp.exp(-0.5 * values * values) * (1.0 / math.sqrt(2.0 * math.pi))
    return normal_cdf + values * density


def mm(a, b):
    return jnp.dot(a, b, preferred_element_type=F32)


class Place:
    def __init__(self):
        self.gx = lax.axis_index("gx")
        self.gy = lax.axis_index("gy")
        self.lo = lax.rem(self.gy, HALF)
        self.hi = lax.div(self.gy, HALF)

    def x_peer(self, d):
        return lax.rem(self.gx + d, GX)

    def y_peer(self, d):
        return lax.rem(self.gy + d, GY)

    def half_peer(self, d):
        return lax.rem(self.lo + d, HALF)

    def greet(self):
        barrier = pltpu.get_barrier_semaphore()
        for d in range(1, GX):
            pl.semaphore_signal(
                barrier, inc=1, device_id={"gx": self.x_peer(d)}, device_id_type=MESH
            )
        for d in range(1, GY):
            pl.semaphore_signal(
                barrier, inc=1, device_id={"gy": self.y_peer(d)}, device_id_type=MESH
            )
        pl.semaphore_wait(barrier, GX + GY - 2)


def remote(src, dst, send, recv, device):
    pltpu.make_async_remote_copy(
        src_ref=src, dst_ref=dst, send_sem=send, recv_sem=recv,
        device_id=device, device_id_type=MESH,
    ).start()


def local(src, dst, sem):
    pltpu.make_async_copy(src, dst, sem).start()


def wait_for(region, sem):
    pltpu.make_async_copy(region, region, sem).wait()


def half_exchange(me, src, dst, send, recv):
    for d in range(1, HALF):
        peer = me.half_peer(d)
        remote(src.at[peer], dst.at[me.lo], send, recv, {"gy": me.hi * HALF + peer})
    local(src.at[me.lo], dst.at[me.lo], recv)


def twin(me, src, dst, send, recv):
    remote(src, dst, send, recv, {"gy": (1 - me.hi) * HALF + me.lo})


def column_exchange(me, src, dst, send, recv):
    for d in range(1, GX):
        peer = me.x_peer(d)
        remote(src.at[peer], dst.at[me.gx], send, recv, {"gx": peer})
    local(src.at[me.gx], dst.at[me.gx], recv)


def column_spread(me, src, dst, send, recv):
    for d in range(1, GX):
        remote(src, dst.at[me.gx], send, recv, {"gx": me.x_peer(d)})
    local(src, dst.at[me.gx], recv)


FORWARD_SCRATCH = [
    pltpu.VMEM((CHUNKS, HALF, 128, KZT), BF),
    pltpu.VMEM((CHUNKS, HALF, 128, KZT), BF),
    pltpu.VMEM((CHUNKS, 2, HALF, 32, KZT), BF),
    pltpu.VMEM((CHUNKS, HALF, 32, KZT), BF),
    pltpu.VMEM((CHUNKS, HALF, 32, KZT), BF),
    pltpu.VMEM((CHUNKS, HALF, 32, KZT), BF),
    pltpu.VMEM((CHUNKS, GX, 64, KZT), BF),
    pltpu.VMEM((CHUNKS, GX, 64, KZT), BF),
    pltpu.SemaphoreType.DMA((4, CHUNKS)),
    pltpu.SemaphoreType.DMA((4, CHUNKS)),
]
INVERSE_SCRATCH = [
    pltpu.VMEM((CHUNKS, GX, 64, KZT), BF),
    pltpu.VMEM((CHUNKS, HALF, 32, KZT), BF),
    pltpu.VMEM((CHUNKS, 2, HALF, 32, KZT), BF),
    pltpu.VMEM((CHUNKS, HALF, 128, KZT), BF),
    pltpu.VMEM((CHUNKS, HALF, 128, KZT), BF),
    pltpu.SemaphoreType.DMA((4, CHUNKS)),
    pltpu.SemaphoreType.DMA((4, CHUNKS)),
]


class Forward:
    def __init__(self, me, depth, yf, xf, out, sa, ra, half, other, sb, rb, sc, rc, send, recv):
        self.me, self.depth, self.yf, self.xf, self.out = me, depth, yf, xf, out
        self.sa, self.ra, self.sb, self.rb, self.sc, self.rc = sa, ra, sb, rb, sc, rc
        self.half, self.other = half, other
        self.send, self.recv = send, recv

    def put(self, c, part, parts, grid):
        count = XL // parts
        modes = mm(grid, self.depth[...])
        real = modes[:, :KZT].reshape(count, CC, 1, YL, KZT)
        imag = modes[:, KZT:].reshape(count, CC, 1, YL, KZT)
        both = jnp.concatenate([real, imag], 2).reshape(count * 64, KZT).astype(BF)
        self.sa[c, pl.ds(part * (count // 2), count // 2)] = both.reshape(count // 2, 128, KZT)

    def send_a(self, c):
        half_exchange(
            self.me, self.sa.at[c], self.ra.at[c], self.send.at[0, c], self.recv.at[0, c]
        )

    def stage_b(self, c):
        wait_for(self.ra.at[c], self.recv.at[0, c])
        for x2 in range(2):
            block = self.ra[c, :, x2 * 64 : x2 * 64 + 64, :].reshape(512, KZT)
            self.half[c, :, :, x2 * 16 : x2 * 16 + 16, :] = (
                mm(self.yf[...], block).astype(BF).reshape(2, HALF, 16, KZT)
            )
        twin(
            self.me, self.half.at[c, 1 - self.me.hi], self.other.at[c],
            self.send.at[1, c], self.recv.at[1, c],
        )

    def stage_e(self, c):
        wait_for(self.other.at[c], self.recv.at[1, c])
        mine = self.half[c, pl.ds(self.me.hi, 1)].reshape(HALF, 32, KZT)
        self.sb[c] = (mine.astype(F32) + self.other[c].astype(F32)).astype(BF)
        half_exchange(
            self.me, self.sb.at[c], self.rb.at[c], self.send.at[2, c], self.recv.at[2, c]
        )

    def stage_c(self, c):
        wait_for(self.rb.at[c], self.recv.at[2, c])
        block = self.rb[c].reshape(256, KZT)
        self.sc[c] = mm(self.xf[...], block).astype(BF).reshape(GX, 64, KZT)
        column_exchange(
            self.me, self.sc.at[c], self.rc.at[c], self.send.at[3, c], self.recv.at[3, c]
        )

    def stage_d(self, c):
        wait_for(self.rc.at[c], self.recv.at[3, c])
        total = self.rc[c, 0].astype(F32)
        for source in range(1, GX):
            total = total + self.rc[c, source].astype(F32)
        for half in range(2):
            lanes = slice(half * 128, half * 128 + 128)
            self.out[c, :, half] = total[:, lanes].reshape(8, 8, 128)

    def finish(self):
        @pl.loop(0, CHUNKS)
        def _(c):
            wait_for(self.sa.at[c, pl.ds(0, HALF - 1)], self.send.at[0, c])
            wait_for(self.other.at[c], self.send.at[1, c])
            wait_for(self.sb.at[c, pl.ds(0, HALF - 1)], self.send.at[2, c])
            wait_for(self.sc.at[c, pl.ds(0, GX - 1)], self.send.at[3, c])


class Inverse:
    def __init__(self, me, back, yi, xi, spec, rp, sq, rq, sr, rr, send, recv):
        self.me, self.back, self.yi, self.xi, self.spec = me, back, yi, xi, spec
        self.rp, self.sq, self.rq, self.sr, self.rr = rp, sq, rq, sr, rr
        self.send, self.recv = send, recv

    def stage_p(self, c):
        column_spread(
            self.me, self.spec.at[c], self.rp.at[c], self.send.at[0, c], self.recv.at[0, c]
        )

    def stage_q(self, c):
        wait_for(self.rp.at[c], self.recv.at[0, c])
        block = self.rp[c].reshape(512, KZT)
        self.sq[c] = mm(self.xi[...], block).astype(BF).reshape(HALF, 32, KZT)
        half_exchange(
            self.me, self.sq.at[c], self.rq.at[c, self.me.hi],
            self.send.at[1, c], self.recv.at[1, c],
        )

    def stage_t(self, c):
        mine = self.rq.at[c, self.me.hi]
        wait_for(mine, self.recv.at[1, c])
        twin(self.me, mine, mine, self.send.at[2, c], self.recv.at[2, c])

    def stage_r(self, c):
        wait_for(self.rq.at[c, 1 - self.me.hi], self.recv.at[2, c])
        for x2 in range(2):
            block = self.rq[c, :, :, x2 * 16 : x2 * 16 + 16, :].reshape(256, KZT)
            self.sr[c, :, x2 * 64 : x2 * 64 + 64, :] = (
                mm(self.yi[...], block).astype(BF).reshape(HALF, 64, KZT)
            )
        half_exchange(
            self.me, self.sr.at[c], self.rr.at[c], self.send.at[3, c], self.recv.at[3, c]
        )

    def ready(self, c):
        wait_for(self.rr.at[c], self.recv.at[3, c])

    def branch(self, c, part, parts):
        count = XL // parts
        block = self.rr[c, pl.ds(part * (count // 2), count // 2)].astype(F32)
        block = block.reshape(count, CC, 2, YL, KZT)
        real = block[:, :, 0].reshape(count * CR, KZT).astype(BF)
        imag = block[:, :, 1].reshape(count * CR, KZT).astype(BF)
        return mm(real, self.back[:KZT, :]) + mm(imag, self.back[KZT:, :])

    def finish(self):
        @pl.loop(0, CHUNKS)
        def _(c):
            wait_for(self.rp.at[c, pl.ds(0, GX - 1)], self.send.at[0, c])
            wait_for(self.sq.at[c, pl.ds(0, HALF - 1)], self.send.at[1, c])
            wait_for(self.sq.at[c], self.send.at[2, c])
            wait_for(self.sr.at[c, pl.ds(0, HALF - 1)], self.send.at[3, c])


def staged(stages, extras=()):
    depth = len(stages)

    @pl.loop(0, CHUNKS + depth - 1)
    def _(t):
        for s, stage in enumerate(stages):
            @pl.when(jnp.logical_and(t >= s, t < CHUNKS + s))
            def _(stage=stage, s=s):
                stage(t - s)
        for step, extra in extras:
            @pl.when(t == step)
            def _(extra=extra):
                extra()


TILES = 10
TILE = (TILES, 8, 128)


def tile_rows():
    return lax.broadcasted_iota(jnp.int32, (8, 128), 0)


def swap_parts(tiles):
    even = (lax.rem(lax.broadcasted_iota(jnp.int32, TILE, 1), 2) == 0)
    return jnp.where(even, pltpu.roll(tiles, 7, 1), pltpu.roll(tiles, 1, 1)), even


def coefficient(modes, kl, i, part):
    row = pl.ds((i % CC) * 2 + part, 1)
    low = jnp.broadcast_to(modes[i // CC, kl, 0, row, :], (8, 128))
    high = jnp.broadcast_to(modes[i // CC, kl, 1, row, :], (8, 128))
    return jnp.where(lax.rem(tile_rows(), 4) < 2, low, high)


def tiles_of(modes, kl, flat):
    for c in range(CHUNKS):
        for half in range(2):
            for part in range(2):
                flat[pl.ds(c * 16 + half * 2 + part, CC, 4), :] = modes[
                    c, kl, half, pl.ds(part, CC, 2), :
                ]
    return flat[...].reshape(TILE)


def pack_halves(values, out):
    for half in range(2):
        lanes = slice(half * 128, half * 128 + 128)
        out[:, :, lanes] = values[:, :, half].reshape(CHUNKS, 64, 128).astype(BF)


def mix_modes(modes, weight, flat, spec, out):
    @pl.loop(0, 8)
    def _(kl):
        by_real = jnp.zeros(TILE, F32)
        by_imag = jnp.zeros(TILE, F32)
        for i in range(C):
            block = weight[kl * C + i].astype(F32).reshape(TILE)
            by_real = by_real + block * coefficient(modes, kl, i, 0)[None]
            by_imag = by_imag + block * coefficient(modes, kl, i, 1)[None]
        turned, even = swap_parts(by_imag)
        flat[...] = (by_real + jnp.where(even, -turned, turned)).reshape(80, 128)
        for c in range(CHUNKS):
            for half in range(2):
                for part in range(2):
                    spec[c, kl, half, pl.ds(part, CC, 2), :] = flat[
                        pl.ds(c * 16 + half * 2 + part, CC, 4), :
                    ]

    pack_halves(spec[...] * mode_weight(spec.shape), out)


def adjoint_modes(scaled, weight, flat, sums, spec, out):
    @pl.loop(0, 8)
    def _(kl):
        grad = tiles_of(scaled, kl, flat)
        turned, even = swap_parts(grad)
        turned = jnp.where(even, turned, -turned)
        for i in range(C):
            block = weight[kl * C + i].astype(F32).reshape(TILE)
            sums[0, i * 8 : i * 8 + 8] = (block * grad).sum(0)
            sums[1, i * 8 : i * 8 + 8] = (block * turned).sum(0)
        for c in range(CHUNKS):
            for half in range(2):
                for part in range(2):
                    total = None
                    for row in (0, 1, 4, 5):
                        term = sums[part, pl.ds(c * 32 + half * 2 + row, CC, 8), :]
                        total = term if total is None else total + term
                    spec[c, kl, half, pl.ds(part, CC, 2), :] = total

    pack_halves(spec[...], out)


def gradient_kernel(modes, scaled, out, flat):
    kl = pl.program_id(0)
    grad = tiles_of(scaled, kl, flat)
    turned, even = swap_parts(grad)
    turned = jnp.where(even, turned, -turned)
    for i in range(C):
        real = coefficient(modes, kl, i, 0)[None]
        imag = coefficient(modes, kl, i, 1)[None]
        out[i] = (grad * real + turned * imag).reshape(80, 128)


def channel_rows():
    rows = lax.broadcasted_iota(jnp.int32, (ROWS, C), 0)
    return lax.div(rows, YL) == lax.broadcasted_iota(jnp.int32, (ROWS, C), 1)


def same_place():
    rows = lax.broadcasted_iota(jnp.int32, (ROWS, ROWS), 0)
    columns = lax.broadcasted_iota(jnp.int32, (ROWS, ROWS), 1)
    return lax.rem(rows, YL) == lax.rem(columns, YL)


def spread_mixer(mixer, axis):
    spread = jnp.where(channel_rows(), 1.0, 0.0).astype(BF)
    half = lax.dot_general(
        spread, mixer, (((1,), (1 - axis,)), ((), ())), preferred_element_type=F32
    ).astype(BF)
    full = lax.dot_general(
        half, spread, (((1,), (1,)), ((), ())), preferred_element_type=F32
    )
    return jnp.where(same_place(), full, 0.0).astype(BF)


FORWARD_TABLES = [
    pltpu.VMEM((NZT, 2 * KZT), BF),
    pltpu.VMEM((256, 512), BF),
    pltpu.VMEM((512, 256), BF),
    pltpu.SemaphoreType.DMA((3,)),
]
INVERSE_TABLES = [
    pltpu.VMEM((2 * KZT, NZT), BF),
    pltpu.VMEM((512, 256), BF),
    pltpu.VMEM((256, 512), BF),
    pltpu.SemaphoreType.DMA((3,)),
]


def fetch_tables(me, depth_hbm, y_hbm, x_hbm, depth, y, x, sem):
    pairs = ((depth_hbm, depth), (y_hbm.at[me.hi], y), (x_hbm.at[me.gx], x))
    for n, (src, dst) in enumerate(pairs):
        local(src, dst, sem.at[n])

    def ready():
        for n, (_, dst) in enumerate(pairs):
            wait_for(dst, sem.at[n])

    return ready


def load_chunks(src, dst, sem):
    @pl.loop(0, CHUNKS)
    def _(c):
        local(src.at[:, pl.ds(c * CR, CR), :], dst.at[c], sem.at[c])


def wait_chunks(dst, sem):
    @pl.loop(0, CHUNKS)
    def _(c):
        wait_for(dst.at[c], sem.at[c])


def first_kernel(
    x_hbm, weight_hbm, depth_hbm, yf_hbm, xf_hbm, modes, spec_out,
    xbuf, weight, flat, spec, xsem, wsem, depth, yf, xf, tsem, *scratch
):
    me = Place()
    load_chunks(x_hbm, xbuf, xsem)
    tables_ready = fetch_tables(me, depth_hbm, yf_hbm, xf_hbm, depth, yf, xf, tsem)
    local(weight_hbm, weight, wsem)
    me.greet()
    fwd = Forward(me, depth, yf, xf, modes, *scratch)
    tables_ready()

    def stage_a(c):
        wait_for(xbuf.at[c], xsem.at[c])
        for part in range(2):
            fwd.put(c, part, 2, xbuf[c, part * 8 : part * 8 + 8].reshape(8 * CR, NZT))
        fwd.send_a(c)

    staged([stage_a, fwd.stage_b, fwd.stage_e, fwd.stage_c, fwd.stage_d])
    wait_for(weight, wsem)
    mix_modes(modes, weight, flat, spec, spec_out)
    fwd.finish()


def second_kernel(
    x_hbm, cot_hbm, weight_hbm, spec_in, mixer, bias,
    depth_hbm, yf_hbm, xf_hbm, back_hbm, yi_hbm, xi_hbm,
    grad_hbm, scaled, spec_out,
    cbuf, gbuf, point, weight, flat, sums, spec, xsem, csem, gsem, wsem, *scratch
):
    me = Place()
    n = len(FORWARD_TABLES)
    depth, yf, xf, tsem, back, yi, xi, isem = scratch[: 2 * n]
    scratch = scratch[2 * n :]
    inverse_ready = fetch_tables(me, back_hbm, yi_hbm, xi_hbm, back, yi, xi, isem)
    load_chunks(x_hbm, gbuf, xsem)
    load_chunks(cot_hbm, cbuf, csem)
    forward_ready = fetch_tables(me, depth_hbm, yf_hbm, xf_hbm, depth, yf, xf, tsem)
    local(weight_hbm, weight, wsem)
    me.greet()
    n = len(INVERSE_SCRATCH)
    inv = Inverse(me, back, yi, xi, spec_in, *scratch[:n])
    fwd = Forward(me, depth, yf, xf, scaled, *scratch[n:])

    @pl.loop(0, CHUNKS)
    def _(c):
        inv.stage_p(c)

    inverse_ready()
    forward_ready()
    wait_chunks(gbuf, xsem)

    def pointwise(part):
        spread = spread_mixer(mixer[...], 0)
        shift = jnp.where(channel_rows(), bias[...], 0.0).sum(1, keepdims=True)

        @pl.loop(part * 8, part * 8 + 8)
        def _(x):
            point[x] = mm(spread, gbuf[:, x].reshape(ROWS, NZT)) + shift

    def stage_s(c):
        inv.ready(c)
        wait_for(cbuf.at[c], csem.at[c])

        @pl.loop(0, 2)
        def _(part):
            rows = pl.ds(part * 8, 8)
            pre = inv.branch(c, part, 2)
            pre = pre + point[rows, pl.ds(c * CR, CR), :].reshape(8 * CR, NZT)
            cot = cbuf[c, rows].reshape(8 * CR, NZT).astype(F32)
            grad = (cot * gelu_slope(pre)).astype(BF)
            gbuf[c, rows] = grad.reshape(8, CR, NZT)
            fwd.put(c, part, 2, grad)

        local(gbuf.at[c], grad_hbm.at[:, pl.ds(c * CR, CR), :], gsem.at[c])
        fwd.send_a(c)

    staged(
        [
            inv.stage_q, inv.stage_t, inv.stage_r, stage_s,
            fwd.stage_b, fwd.stage_e, fwd.stage_c, fwd.stage_d,
        ],
        [(0, lambda: pointwise(0)), (1, lambda: pointwise(1))],
    )
    scaled[...] = scaled[...] * mode_weight(scaled.shape)
    wait_for(weight, wsem)
    adjoint_modes(scaled, weight, flat, sums, spec, spec_out)
    wait_chunks(gbuf, gsem)
    inv.finish()
    fwd.finish()


def third_kernel(
    x_hbm, grad_hbm, spec_in, mixer, back_hbm, yi_hbm, xi_hbm, out_hbm, mixer_out, bias_out,
    xbuf, gbuf, obuf, point, mixed, one, col, two, row, xsem, gsem, osem, small, *scratch
):
    me = Place()
    n = len(INVERSE_TABLES)
    back, yi, xi, isem = scratch[:n]
    inverse_ready = fetch_tables(me, back_hbm, yi_hbm, xi_hbm, back, yi, xi, isem)
    local(x_hbm, xbuf, xsem)
    local(grad_hbm, gbuf, gsem)
    me.greet()
    inv = Inverse(me, back, yi, xi, spec_in, *scratch[n:])

    @pl.loop(0, CHUNKS)
    def _(c):
        inv.stage_p(c)

    inverse_ready()
    wait_for(xbuf, xsem)
    wait_for(gbuf, gsem)
    mixed[...] = jnp.zeros_like(mixed)

    def pointwise(part):
        spread = spread_mixer(mixer[...], 1)
        contract = (((1,), (1,)), ((), ()))

        @pl.loop(part * 8, part * 8 + 8)
        def _(x):
            grad = gbuf[x]
            point[x] = mm(spread, grad)
            mixed[:ROWS, :] += lax.dot_general(
                xbuf[x], grad, contract, preferred_element_type=F32
            )
            mixed[ROWS:, :] += lax.dot_general(
                jnp.ones((8, NZT), BF), grad, contract, preferred_element_type=F32
            )

    def second_half():
        pointwise(1)
        kept = jnp.where(same_place(), mixed[:ROWS, :], 0.0).reshape(C, YL, ROWS).sum(1)
        stacked = jnp.concatenate([kept, mixed[ROWS : ROWS + 4, :]], 0)
        fold = lax.div(lax.broadcasted_iota(jnp.int32, (ROWS, 128), 0), YL)
        fold = fold == lax.broadcasted_iota(jnp.int32, (ROWS, 128), 1)
        one[...] = lax.dot_general(
            stacked, jnp.where(fold, 1.0, 0.0), (((1,), (0,)), ((), ())),
            precision=lax.Precision.HIGHEST, preferred_element_type=F32,
        )
        for d in range(1, GX):
            remote(one, col.at[me.gx], small.at[0], small.at[1], {"gx": me.x_peer(d)})
        local(one, col.at[me.gx], small.at[1])

    def across_rows():
        wait_for(col, small.at[1])
        total = col[0]
        for source in range(1, GX):
            total = total + col[source]
        two[...] = total
        for d in range(1, GY):
            remote(two, row.at[me.gy], small.at[2], small.at[3], {"gy": me.y_peer(d)})
        local(two, row.at[me.gy], small.at[3])

    def stage_s(c):
        inv.ready(c)

        @pl.loop(0, 2)
        def _(part):
            rows = pl.ds(part * 8, 8)
            total = inv.branch(c, part, 2)
            total = total + point[rows, pl.ds(c * CR, CR), :].reshape(8 * CR, NZT)
            obuf[c, rows] = total.astype(BF).reshape(8, CR, NZT)

        local(obuf.at[c], out_hbm.at[:, pl.ds(c * CR, CR), :], osem.at[c])

    staged(
        [inv.stage_q, inv.stage_t, inv.stage_r, stage_s],
        [(0, lambda: pointwise(0)), (1, second_half), (3, across_rows)],
    )
    wait_for(row, small.at[3])
    total = row[0]
    for source in range(1, GY):
        total = total + row[source]
    total = total * (1.0 / math.sqrt(NX * NY * NZT))
    mixer_out[...] = total[:C, :C]
    bias_out[...] = total[C : C + 1, :C]
    wait_for(col.at[pl.ds(0, GX - 1)], small.at[0])
    wait_for(row.at[pl.ds(0, GY - 1)], small.at[2])
    wait_chunks(obuf, osem)
    inv.finish()


ANY = pl.BlockSpec(memory_space=pl.ANY)
VM = pl.BlockSpec(memory_space=pltpu.VMEM)


def params(number):
    return pltpu.CompilerParams(
        collective_id=number, has_side_effects=True, vmem_limit_bytes=60 * 2**20
    )


def body(layer_input, cotangent, spectral_weight, mixer_weight, bias_vector):
    depth, back, yf, yi, xf, xi = (jnp.asarray(v) for v in tables())
    grid = jnp.swapaxes(layer_input, 1, 2).reshape(XL, ROWS, NZT)
    cot = jnp.swapaxes(cotangent, 1, 2).reshape(XL, ROWS, NZT)
    weight = spectral_weight.reshape(8 * C, C, 2, 2, 128)
    weight = jnp.swapaxes(weight, 2, 3).reshape(8 * C, 4 * C, 128)
    modes_f32 = jax.ShapeDtypeStruct((CHUNKS, 8, 2, 8, 128), F32)
    modes_bf16 = jax.ShapeDtypeStruct((CHUNKS, 64, KZT), BF)
    field = jax.ShapeDtypeStruct((XL, ROWS, NZT), BF)
    chunked = pltpu.VMEM((CHUNKS, XL, CR, NZT), BF)
    chunk_sems = pltpu.SemaphoreType.DMA((CHUNKS,))
    weights_held = pltpu.VMEM((8 * C, 4 * C, 128), BF)
    flat = pltpu.VMEM((4 * C, 128), F32)
    spec_held = pltpu.VMEM((CHUNKS, 8, 2, 8, 128), F32)

    modes, spectrum = pl.pallas_call(
        first_kernel,
        out_shape=[modes_f32, modes_bf16],
        in_specs=[ANY] * 5,
        out_specs=[VM, VM],
        scratch_shapes=[
            chunked, weights_held, flat, spec_held, chunk_sems, pltpu.SemaphoreType.DMA,
        ]
        + FORWARD_TABLES
        + FORWARD_SCRATCH,
        compiler_params=params(1),
        name="first",
    )(grid, weight, depth, yf, xf)

    pre_grad, scaled, grad_spectrum = pl.pallas_call(
        second_kernel,
        out_shape=[field, modes_f32, modes_bf16],
        in_specs=[ANY, ANY, ANY] + [VM] * 3 + [ANY] * 6,
        out_specs=[ANY, VM, VM],
        scratch_shapes=[
            chunked, chunked, pltpu.VMEM((XL, ROWS, NZT), F32), weights_held, flat,
            pltpu.VMEM((2, 8 * C, 128), F32), spec_held,
            chunk_sems, chunk_sems, chunk_sems, pltpu.SemaphoreType.DMA,
        ]
        + FORWARD_TABLES
        + INVERSE_TABLES
        + INVERSE_SCRATCH
        + FORWARD_SCRATCH,
        compiler_params=params(2),
        name="second",
    )(
        grid, cot, weight, spectrum, mixer_weight, bias_vector.reshape(1, C),
        depth, yf, xf, back, yi, xi,
    )

    spectral_grad = pl.pallas_call(
        gradient_kernel,
        out_shape=jax.ShapeDtypeStruct((8 * C, 4 * C, 128), F32),
        grid=(8,),
        in_specs=[pl.BlockSpec((CHUNKS, 8, 2, 8, 128), lambda kl: (0, 0, 0, 0, 0))] * 2,
        out_specs=pl.BlockSpec((C, 4 * C, 128), lambda kl: (kl, 0, 0)),
        scratch_shapes=[flat],
        name="gradient",
    )(modes, scaled)
    spectral_grad = jnp.swapaxes(spectral_grad.reshape(8 * C, C, 2, 2, 128), 2, 3)
    spectral_grad = spectral_grad.reshape(4, 2, C, C, 2, KZT)

    input_grad, mixer_grad, bias_grad = pl.pallas_call(
        third_kernel,
        out_shape=[
            field, jax.ShapeDtypeStruct((C, C), F32), jax.ShapeDtypeStruct((1, C), F32),
        ],
        in_specs=[ANY, ANY, VM, VM] + [ANY] * 3,
        out_specs=[ANY, VM, VM],
        scratch_shapes=[
            pltpu.VMEM((XL, ROWS, NZT), BF),
            pltpu.VMEM((XL, ROWS, NZT), BF),
            chunked,
            pltpu.VMEM((XL, ROWS, NZT), F32),
            pltpu.VMEM((ROWS + 8, ROWS), F32),
            pltpu.VMEM((24, 128), F32),
            pltpu.VMEM((GX, 24, 128), F32),
            pltpu.VMEM((24, 128), F32),
            pltpu.VMEM((GY, 24, 128), F32),
            pltpu.SemaphoreType.DMA,
            pltpu.SemaphoreType.DMA,
            chunk_sems,
            pltpu.SemaphoreType.DMA((4,)),
        ]
        + INVERSE_TABLES
        + INVERSE_SCRATCH,
        compiler_params=params(3),
        name="third",
    )(grid, pre_grad, grad_spectrum, mixer_weight, back, yi, xi)
    input_grad = jnp.swapaxes(input_grad.reshape(XL, C, YL, NZT), 1, 2)
    return (input_grad, spectral_grad, mixer_grad, bias_grad.reshape(C))


def solution(mesh):
    return jax.shard_map(
        body,
        mesh=mesh,
        in_specs=(
            P("gx", "gy", None, None),
            P("gx", "gy", None, None),
            P("gx", "gy", None, None, None, None),
            P(),
            P(),
        ),
        out_specs=(P("gx", "gy", None, None), P("gx", "gy", None, None, None, None), P(), P()),
        check_vma=False,
    )
```

```python
import functools
import math

import jax
import jax.numpy as jnp
import ml_dtypes
import numpy as np
from jax import lax
from jax.experimental import pallas as pl
from jax.experimental.pallas import tpu as pltpu
from jax.sharding import PartitionSpec as P

NX = 128
NY = 128
NZ = 64
NT = 16
C = 20
MZ = 16
MT = 8
KX = 32
KY = 32
KZT = 256
NZT = 1024
GX = 8
GY = 16
HALF = 8
XL = NX // GX
YL = NY // GY
CHUNKS = 5
CC = C // CHUNKS
ROWS = C * YL
CR = CC * YL
BF = jnp.bfloat16
F32 = jnp.float32
MESH = pl.DeviceIdType.MESH


def signed_frequency(number):
    values = np.arange(number)
    return np.where(values < number // 2, values, values - number)


def pair_table(frequency, length):
    places = np.arange(length)
    phases = np.mod(frequency[:, None] * places[None, :], length)
    angles = phases * (-2.0 * math.pi / length)
    factor = float(length) ** (-0.5)
    cosine = np.cos(angles) * factor
    sine_part = np.sin(angles) * factor
    top_rows = np.stack([cosine, -sine_part], -1)
    low_rows = np.stack([sine_part, cosine], -1)
    return np.stack([top_rows, low_rows], 1)


def depth_table():
    fz = signed_frequency(2 * MZ)
    ft = np.arange(MT)
    z = np.arange(NZ)
    t = np.arange(NT)
    phases = (
        z[:, None, None, None] * fz[None, None, :, None] * NT
        + t[None, :, None, None] * ft[None, None, None, :] * NZ
    )
    phases = np.mod(phases, NZT).reshape(NZT, KZT)
    angles = phases * (-2.0 * math.pi / NZT)
    factor = float(NZT) ** (-0.5)
    stacked = np.stack([np.cos(angles) * factor, np.sin(angles) * factor], 1)
    return stacked.reshape(NZT, 2 * KZT)


def as_bf16(table):
    return np.ascontiguousarray(table).astype(np.float32).astype(ml_dtypes.bfloat16)


@functools.lru_cache(maxsize=None)
def tables():
    depth = depth_table()
    by_half = np.moveaxis(depth.reshape(NZT, 2, 2, 128), 2, 0).reshape(2, NZT, 256)
    xt = pair_table(signed_frequency(KX), NX)
    yt = pair_table(signed_frequency(KY), NY)
    eye = np.eye(2)
    yv = yt.reshape(GY, 2, 2, 2, HALF, YL, 2)
    yf = np.einsum("jlphsyq,cd,ab->hjalcpsbdqy", yv, eye, eye).reshape(2, 256, 512)
    xv = xt.reshape(GX, 4, 2, GX, HALF, 2, 2)
    xf = np.einsum("iapgsxq,cd,lm->gialcpsxmdq", xv, eye, eye).reshape(GX, 256, 128)
    yi = np.transpose(yf, (0, 2, 1))
    xi = np.transpose(xf, (0, 2, 1))
    return tuple(as_bf16(v) for v in (by_half, depth.T, yf, yi, xf, xi))


def mode_weight(shape):
    lanes = lax.broadcasted_iota(jnp.int32, shape, len(shape) - 1)
    return jnp.where(lax.rem(lanes, MT) == 0, 1.0, 2.0).astype(F32)


def gelu_slope(values):
    normal_cdf = 0.5 * (1.0 + lax.erf(values * (1.0 / math.sqrt(2.0))))
    density = jnp.exp(-0.5 * values * values) * (1.0 / math.sqrt(2.0 * math.pi))
    return normal_cdf + values * density


def mm(a, b):
    return jnp.dot(a, b, preferred_element_type=F32)


class Place:
    def __init__(self):
        self.gx = lax.axis_index("gx")
        self.gy = lax.axis_index("gy")
        self.lo = lax.rem(self.gy, HALF)
        self.hi = lax.div(self.gy, HALF)

    def x_peer(self, d):
        return lax.rem(self.gx + d, GX)

    def y_peer(self, d):
        return lax.rem(self.gy + d, GY)

    def half_peer(self, d):
        return lax.rem(self.lo + d, HALF)

    def greet(self):
        barrier = pltpu.get_barrier_semaphore()
        for d in range(1, GX):
            pl.semaphore_signal(
                barrier, inc=1, device_id={"gx": self.x_peer(d)}, device_id_type=MESH
            )
        for d in range(1, GY):
            pl.semaphore_signal(
                barrier, inc=1, device_id={"gy": self.y_peer(d)}, device_id_type=MESH
            )
        pl.semaphore_wait(barrier, GX + GY - 2)


def remote(src, dst, send, recv, device):
    pltpu.make_async_remote_copy(
        src_ref=src, dst_ref=dst, send_sem=send, recv_sem=recv,
        device_id=device, device_id_type=MESH,
    ).start()


def local(src, dst, sem):
    pltpu.make_async_copy(src, dst, sem).start()


def wait_for(region, sem):
    pltpu.make_async_copy(region, region, sem).wait()


def half_exchange(me, src, dst, send, recv):
    for d in range(1, HALF):
        peer = me.half_peer(d)
        remote(src.at[peer], dst.at[me.lo], send, recv, {"gy": me.hi * HALF + peer})
    local(src.at[me.lo], dst.at[me.lo], recv)


def twin(me, src, dst, send, recv):
    remote(src, dst, send, recv, {"gy": (1 - me.hi) * HALF + me.lo})


def column_exchange(me, src, dst, send, recv):
    for d in range(1, GX):
        peer = me.x_peer(d)
        remote(src.at[peer], dst.at[me.gx], send, recv, {"gx": peer})
    local(src.at[me.gx], dst.at[me.gx], recv)


def column_spread(me, src, dst, send, recv):
    for d in range(1, GX):
        remote(src, dst.at[me.gx], send, recv, {"gx": me.x_peer(d)})
    local(src, dst.at[me.gx], recv)


UNITS = 2 * CHUNKS
SLACK = (2, 2, 2, 2, 2, 2, 2, 2)
FORWARD_SCRATCH = [
    pltpu.VMEM((UNITS, HALF, 64, KZT), BF),
    pltpu.VMEM((UNITS, HALF, 64, KZT), BF),
    pltpu.VMEM((UNITS, 2, HALF, 16, KZT), BF),
    pltpu.VMEM((UNITS, HALF, 16, KZT), BF),
    pltpu.VMEM((UNITS, HALF, 16, KZT), BF),
    pltpu.VMEM((UNITS, HALF, 16, KZT), BF),
    pltpu.VMEM((UNITS, GX, 32, KZT), BF),
    pltpu.VMEM((UNITS, GX, 32, KZT), BF),
    pltpu.SemaphoreType.DMA((4, UNITS)),
    pltpu.SemaphoreType.DMA((4, UNITS)),
]
INVERSE_SCRATCH = [
    pltpu.VMEM((UNITS, 32, KZT), BF),
    pltpu.VMEM((UNITS, GX, 32, KZT), BF),
    pltpu.VMEM((UNITS, HALF, 16, KZT), BF),
    pltpu.VMEM((UNITS, 2, HALF, 16, KZT), BF),
    pltpu.VMEM((UNITS, HALF, 64, KZT), BF),
    pltpu.VMEM((UNITS, HALF, 64, KZT), BF),
    pltpu.SemaphoreType.DMA((4, UNITS)),
    pltpu.SemaphoreType.DMA((4, UNITS)),
]


class Forward:
    def __init__(self, me, depth, yf, xf, sa, ra, half, other, sb, rb, sc, rc, send, recv):
        self.me, self.depth, self.yf, self.xf = me, depth, yf, xf
        self.sa, self.ra, self.sb, self.rb, self.sc, self.rc = sa, ra, sb, rb, sc, rc
        self.half, self.other = half, other
        self.send, self.recv = send, recv

    def sent_a(self, u):
        wait_for(self.sa.at[u, pl.ds(0, HALF - 1)], self.send.at[0, u])

    def sent_b(self, u):
        wait_for(self.other.at[u], self.send.at[1, u])

    def sent_e(self, u):
        wait_for(self.sb.at[u, pl.ds(0, HALF - 1)], self.send.at[2, u])

    def sent_c(self, u):
        wait_for(self.sc.at[u, pl.ds(0, GX - 1)], self.send.at[3, u])

    def put(self, u, table, part, parts, grid):
        count = XL // parts
        modes = mm(grid, table)
        real = modes[:, :128].reshape(count, 2, 2, 1, YL, 128)
        imag = modes[:, 128:].reshape(count, 2, 2, 1, YL, 128)
        both = jnp.concatenate([real, imag], 3)
        both = jnp.concatenate([both[:, 0], both[:, 1]], -1).reshape(count * 32, KZT)
        self.sa[u, pl.ds(part * (count // 2), count // 2)] = both.astype(BF).reshape(
            count // 2, 64, KZT
        )

    def send_a(self, u):
        half_exchange(
            self.me, self.sa.at[u], self.ra.at[u], self.send.at[0, u], self.recv.at[0, u]
        )

    def stage_b(self, u, again):
        wait_for(self.ra.at[u], self.recv.at[0, u])
        if again:
            self.sent_b(u)
        block = self.ra[u].reshape(512, KZT)
        self.half[u] = mm(self.yf[...], block).astype(BF).reshape(2, HALF, 16, KZT)
        twin(
            self.me, self.half.at[u, 1 - self.me.hi], self.other.at[u],
            self.send.at[1, u], self.recv.at[1, u],
        )

    def stage_e(self, u, again):
        wait_for(self.other.at[u], self.recv.at[1, u])
        if again:
            self.sent_e(u)
        mine = self.half[u, pl.ds(self.me.hi, 1)].reshape(HALF, 16, KZT)
        self.sb[u] = (mine.astype(F32) + self.other[u].astype(F32)).astype(BF)
        half_exchange(
            self.me, self.sb.at[u], self.rb.at[u], self.send.at[2, u], self.recv.at[2, u]
        )

    def stage_c(self, u, again):
        wait_for(self.rb.at[u], self.recv.at[2, u])
        if again:
            self.sent_c(u)
        block = self.rb[u].reshape(128, KZT)
        self.sc[u] = mm(self.xf[...], block).astype(BF).reshape(GX, 32, KZT)
        column_exchange(
            self.me, self.sc.at[u], self.rc.at[u], self.send.at[3, u], self.recv.at[3, u]
        )

    def stage_d(self, u, out, weighted):
        wait_for(self.rc.at[u], self.recv.at[3, u])
        total = self.rc[u, 0].astype(F32)
        for source in range(1, GX):
            total = total + self.rc[u, source].astype(F32)
        if weighted:
            total = total * mode_weight(total.shape)
        for kl in range(8):
            for pair in range(2):
                out[u, kl, pair * 4 : pair * 4 + 4, :] = total[
                    kl * 4 : kl * 4 + 4, pair * 128 : pair * 128 + 128
                ]

    def finish(self):
        @pl.loop(0, UNITS)
        def _(u):
            self.sent_a(u)
            self.sent_b(u)
            self.sent_e(u)
            self.sent_c(u)


class Inverse:
    def __init__(self, me, back, yi, xi, spec, rp, sq, rq, sr, rr, send, recv):
        self.me, self.back, self.yi, self.xi, self.spec = me, back, yi, xi, spec
        self.rp, self.sq, self.rq, self.sr, self.rr = rp, sq, rq, sr, rr
        self.send, self.recv = send, recv

    def sent_p(self, u):
        wait_for(self.rp.at[u, pl.ds(0, GX - 1)], self.send.at[0, u])

    def sent_q(self, u):
        wait_for(self.sq.at[u, pl.ds(0, HALF - 1)], self.send.at[1, u])

    def sent_r(self, u):
        wait_for(self.sr.at[u, pl.ds(0, HALF - 1)], self.send.at[3, u])

    def start(self, half, spec, unit, again):
        for c in range(CHUNKS):
            u = half * CHUNKS + c
            for kl in range(8):
                for pair in range(2):
                    unit[kl * 4 : kl * 4 + 4, pair * 128 : pair * 128 + 128] = spec[
                        c, kl, pair * 4 : pair * 4 + 4, :
                    ]
            if again:
                self.sent_p(u)
            self.spec[u] = unit[...].astype(BF)

        @pl.loop(half * CHUNKS, half * CHUNKS + CHUNKS)
        def _(u):
            column_spread(
                self.me, self.spec.at[u], self.rp.at[u], self.send.at[0, u], self.recv.at[0, u]
            )

    def stage_q(self, u, again):
        wait_for(self.rp.at[u], self.recv.at[0, u])
        if again:
            self.sent_q(u)
        block = self.rp[u].reshape(256, KZT)
        self.sq[u] = mm(self.xi[...], block).astype(BF).reshape(HALF, 16, KZT)
        half_exchange(
            self.me, self.sq.at[u], self.rq.at[u, self.me.hi],
            self.send.at[1, u], self.recv.at[1, u],
        )

    def stage_t(self, u):
        mine = self.rq.at[u, self.me.hi]
        wait_for(mine, self.recv.at[1, u])
        twin(self.me, mine, mine, self.send.at[2, u], self.recv.at[2, u])

    def stage_r(self, u, again):
        wait_for(self.rq.at[u, 1 - self.me.hi], self.recv.at[2, u])
        wait_for(self.sq.at[u], self.send.at[2, u])
        if again:
            self.sent_r(u)
        block = self.rq[u].reshape(256, KZT)
        self.sr[u] = mm(self.yi[...], block).astype(BF).reshape(HALF, 64, KZT)
        half_exchange(
            self.me, self.sr.at[u], self.rr.at[u], self.send.at[3, u], self.recv.at[3, u]
        )

    def ready(self, c):
        for half in range(2):
            u = half * CHUNKS + c
            wait_for(self.rr.at[u], self.recv.at[3, u])

    def branch(self, c, part, parts):
        count = XL // parts
        total = None
        for p in range(2):
            halves = []
            for half in range(2):
                block = self.rr[half * CHUNKS + c, pl.ds(part * (count // 2), count // 2)]
                block = block.astype(F32).reshape(count, 2, 2, YL, KZT)[:, :, p]
                block = [block[:, None, :, :, :128], block[:, None, :, :, 128:]]
                halves.append(jnp.concatenate(block, 1))
            lhs = jnp.concatenate(halves, -1).reshape(count * CR, KZT).astype(BF)
            term = mm(lhs, self.back[p * KZT : p * KZT + KZT, :])
            total = term if total is None else total + term
        return total

    def finish(self):
        @pl.loop(0, UNITS)
        def _(u):
            self.sent_p(u)
            self.sent_q(u)
            self.sent_r(u)


def run(schedule):
    steps = max(start + count for start, count, _ in schedule)

    @pl.loop(0, steps)
    def _(t):
        for start, count, stage in schedule:
            @pl.when(jnp.logical_and(t >= start, t < start + count))
            def _(stage=stage, start=start):
                stage(t - start)


TILES = 10
TILE = (TILES, 8, 128)


def swap_parts(tiles):
    even = (lax.rem(lax.broadcasted_iota(jnp.int32, TILE, 1), 2) == 0)
    return jnp.where(even, pltpu.roll(tiles, 7, 1), pltpu.roll(tiles, 1, 1)), even


def coefficient(modes, half, kl, i, part):
    row = pl.ds((i % CC) * 2 + part, 1)
    return jnp.broadcast_to(modes[half * CHUNKS + i // CC, kl, row, :], (8, 128))


def lay_out(modes, half, kl, flat):
    for c in range(CHUNKS):
        for part in range(2):
            flat[pl.ds(c * 16 + half * 2 + part, CC, 4), :] = modes[
                half * CHUNKS + c, kl, pl.ds(part, CC, 2), :
            ]


def mix_modes(modes, half, weight, flat, spec):
    @pl.loop(0, 8)
    def _(kl):
        by_real = jnp.zeros(TILE, F32)
        by_imag = jnp.zeros(TILE, F32)
        for i in range(C):
            block = weight[kl * C + i].astype(F32).reshape(TILE)
            by_real = by_real + block * coefficient(modes, half, kl, i, 0)[None]
            by_imag = by_imag + block * coefficient(modes, half, kl, i, 1)[None]
        turned, even = swap_parts(by_imag)
        mixed = by_real + jnp.where(even, -turned, turned)
        flat[...] = (mixed * mode_weight(TILE)).reshape(80, 128)
        for c in range(CHUNKS):
            for part in range(2):
                spec[c, kl, pl.ds(part, CC, 2), :] = flat[
                    pl.ds(c * 16 + half * 2 + part, CC, 4), :
                ]


def adjoint_modes(scaled, half, weight, flat, sums, spec):
    @pl.loop(0, 8)
    def _(kl):
        lay_out(scaled, half, kl, flat)
        grad = flat[...].reshape(TILE)
        turned, even = swap_parts(grad)
        turned = jnp.where(even, turned, -turned)
        for i in range(C):
            block = weight[kl * C + i].astype(F32).reshape(TILE)
            sums[0, i * 8 : i * 8 + 8] = (block * grad).sum(0)
            sums[1, i * 8 : i * 8 + 8] = (block * turned).sum(0)
        for c in range(CHUNKS):
            for part in range(2):
                total = None
                for row in (0, 1, 4, 5):
                    term = sums[part, pl.ds(c * 32 + half * 2 + row, CC, 8), :]
                    total = term if total is None else total + term
                spec[c, kl, pl.ds(part, CC, 2), :] = total


def gradient_kernel(modes, scaled, field, mixer, bias, out, field_out, mixer_out, bias_out, flat):
    field_out[...] = field[...]
    mixer_out[...] = mixer[...]
    bias_out[...] = bias[...]
    kl = pl.program_id(0)
    for half in range(2):
        lay_out(scaled, half, kl, flat)
    grad = flat[...].reshape(TILE)
    turned, even = swap_parts(grad)
    turned = jnp.where(even, turned, -turned)
    first = lax.rem(lax.broadcasted_iota(jnp.int32, (8, 128), 0), 4) < 2
    for i in range(C):
        real, imag = (
            jnp.where(first, coefficient(modes, 0, kl, i, p), coefficient(modes, 1, kl, i, p))
            for p in range(2)
        )
        out[i] = (grad * real[None] + turned * imag[None]).reshape(80, 128)


def channel_rows():
    rows = lax.broadcasted_iota(jnp.int32, (ROWS, C), 0)
    return lax.div(rows, YL) == lax.broadcasted_iota(jnp.int32, (ROWS, C), 1)


def same_place():
    rows = lax.broadcasted_iota(jnp.int32, (ROWS, ROWS), 0)
    columns = lax.broadcasted_iota(jnp.int32, (ROWS, ROWS), 1)
    return lax.rem(rows, YL) == lax.rem(columns, YL)


def spread_mixer(mixer, axis):
    spread = jnp.where(channel_rows(), 1.0, 0.0).astype(BF)
    half = lax.dot_general(
        spread, mixer, (((1,), (1 - axis,)), ((), ())), preferred_element_type=F32
    ).astype(BF)
    full = lax.dot_general(
        half, spread, (((1,), (1,)), ((), ())), preferred_element_type=F32
    )
    return jnp.where(same_place(), full, 0.0).astype(BF)


FORWARD_TABLES = [
    pltpu.VMEM((2, NZT, KZT), BF),
    pltpu.VMEM((256, 512), BF),
    pltpu.VMEM((256, 128), BF),
    pltpu.SemaphoreType.DMA((3,)),
]
INVERSE_TABLES = [
    pltpu.VMEM((2 * KZT, NZT), BF),
    pltpu.VMEM((512, 256), BF),
    pltpu.VMEM((128, 256), BF),
    pltpu.SemaphoreType.DMA((3,)),
]


def fetch_tables(me, depth_hbm, y_hbm, x_hbm, depth, y, x, sem):
    pairs = ((depth_hbm, depth), (y_hbm.at[me.hi], y), (x_hbm.at[me.gx], x))
    for n, (src, dst) in enumerate(pairs):
        local(src, dst, sem.at[n])

    def ready():
        for n, (_, dst) in enumerate(pairs):
            wait_for(dst, sem.at[n])

    return ready


def whole_kernel(
    x_hbm, cot_hbm, weight_hbm, mixer, bias, depth_hbm, yf_hbm, xf_hbm, back_hbm, yi_hbm, xi_hbm,
    out_hbm, modes, scaled, mixer_out, bias_out,
    gbuf, cbuf, point, weight, flat, sums, spec, unit, mixed, one, col, two, row,
    gsem, csem, wsem, small, *scratch
):
    me = Place()
    n = len(FORWARD_TABLES)
    depth, yf, xf, tsem, back, yi, xi, isem = scratch[: 2 * n]
    scratch = scratch[2 * n :]

    def chunk_of(ref, c):
        return ref.at[:, pl.ds(c * CR, CR), :]

    local(chunk_of(x_hbm, 0), gbuf.at[0], gsem.at[0])
    forward_ready = fetch_tables(me, depth_hbm, yf_hbm, xf_hbm, depth, yf, xf, tsem)

    @pl.loop(1, CHUNKS)
    def _(c):
        local(chunk_of(x_hbm, c), gbuf.at[c], gsem.at[c])

    local(weight_hbm, weight, wsem)
    inverse_ready = fetch_tables(me, back_hbm, yi_hbm, xi_hbm, back, yi, xi, isem)

    @pl.loop(0, CHUNKS)
    def _(c):
        local(chunk_of(cot_hbm, c), cbuf.at[c], csem.at[c])

    me.greet()
    n = len(INVERSE_SCRATCH)
    inv = Inverse(me, back, yi, xi, *scratch[:n])
    fwd = Forward(me, depth, yf, xf, *scratch[n:])
    flat[...] = jnp.zeros_like(flat)
    mixed[...] = jnp.zeros_like(mixed)
    forward_ready()

    def first_a(u):
        c = lax.rem(u, CHUNKS)

        @pl.when(u < CHUNKS)
        def _():
            wait_for(gbuf.at[c], gsem.at[c])

        table = depth[lax.div(u, CHUNKS)]
        for part in range(2):
            fwd.put(u, table, part, 2, gbuf[c, part * 8 : part * 8 + 8].reshape(8 * CR, NZT))
        fwd.send_a(u)

    def spectrum(half):
        if half == 0:
            wait_for(weight, wsem)
            inverse_ready()
        mix_modes(modes, half, weight, flat, spec)
        inv.start(half, spec, unit, False)

    def back_spectrum(half):
        adjoint_modes(scaled, half, weight, flat, sums, spec)
        inv.start(half, spec, unit, True)

    def pointwise(n):
        spread = spread_mixer(mixer[...], 0)
        shift = jnp.where(channel_rows(), bias[...], 0.0).sum(1, keepdims=True)
        for x in (2 * n, 2 * n + 1):
            point[x] = mm(spread, gbuf[:, x].reshape(ROWS, NZT)) + shift

    def slope(c):
        inv.ready(c)
        wait_for(cbuf.at[c], csem.at[c])
        fwd.sent_a(c)
        fwd.sent_a(CHUNKS + c)

        @pl.loop(0, 2)
        def _(part):
            rows = pl.ds(part * 8, 8)
            pre = inv.branch(c, part, 2)
            pre = pre + point[rows, pl.ds(c * CR, CR), :].reshape(8 * CR, NZT)
            cot = cbuf[c, rows].reshape(8 * CR, NZT).astype(F32)
            grad = (cot * gelu_slope(pre)).astype(BF)
            gbuf[c, rows] = grad.reshape(8, CR, NZT)
            for half in range(2):
                fwd.put(half * CHUNKS + c, depth[half], part, 2, grad)

        local(chunk_of(x_hbm, c), cbuf.at[c], csem.at[c])

    def pointwise_back(n):
        @pl.when(n == 0)
        def _():
            @pl.loop(0, CHUNKS)
            def _(c):
                wait_for(cbuf.at[c], csem.at[c])

        spread = spread_mixer(mixer[...], 1)
        contract = (((1,), (1,)), ((), ()))
        for x in (2 * n, 2 * n + 1):
            grad = gbuf[:, x].reshape(ROWS, NZT)
            point[x] = mm(spread, grad)
            mixed[:ROWS, :] += lax.dot_general(
                cbuf[:, x].reshape(ROWS, NZT), grad, contract, preferred_element_type=F32
            )
            mixed[ROWS:, :] += lax.dot_general(
                jnp.ones((8, NZT), BF), grad, contract, preferred_element_type=F32
            )

    def across_columns(_):
        kept = jnp.where(same_place(), mixed[:ROWS, :], 0.0).reshape(C, YL, ROWS).sum(1)
        stacked = jnp.concatenate([kept, mixed[ROWS : ROWS + 4, :]], 0)
        fold = lax.div(lax.broadcasted_iota(jnp.int32, (ROWS, 128), 0), YL)
        fold = fold == lax.broadcasted_iota(jnp.int32, (ROWS, 128), 1)
        one[...] = lax.dot_general(
            stacked, jnp.where(fold, 1.0, 0.0), (((1,), (0,)), ((), ())),
            precision=lax.Precision.HIGHEST, preferred_element_type=F32,
        )
        for d in range(1, GX):
            remote(one, col.at[me.gx], small.at[0], small.at[1], {"gx": me.x_peer(d)})
        local(one, col.at[me.gx], small.at[1])

    def across_rows(_):
        wait_for(col, small.at[1])
        total = col[0]
        for source in range(1, GX):
            total = total + col[source]
        two[...] = total
        for d in range(1, GY):
            remote(two, row.at[me.gy], small.at[2], small.at[3], {"gy": me.y_peer(d)})
        local(two, row.at[me.gy], small.at[3])

    def result(c):
        inv.ready(c)

        @pl.loop(0, 2)
        def _(part):
            rows = pl.ds(part * 8, 8)
            total = inv.branch(c, part, 2)
            total = total + point[rows, pl.ds(c * CR, CR), :].reshape(8 * CR, NZT)
            gbuf[c, rows] = total.astype(BF).reshape(8, CR, NZT)

        local(gbuf.at[c], chunk_of(out_hbm, c), gsem.at[c])

    send_b, send_e, send_c, send_d, send_q, send_t, send_r, send_s = SLACK
    at_b = send_b
    at_e = at_b + send_e
    at_c = at_e + send_c
    at_d = at_c + send_d
    at_p = at_d + CHUNKS - 1
    at_q = at_p + send_q
    at_t = at_q + send_t
    at_r = at_t + send_r
    at_s = at_r + CHUNKS + send_s
    run([
        (0, UNITS, first_a),
        (at_b, UNITS, lambda u: fwd.stage_b(u, False)),
        (at_e, UNITS, lambda u: fwd.stage_e(u, False)),
        (at_c, UNITS, lambda u: fwd.stage_c(u, False)),
        (at_d, UNITS, lambda u: fwd.stage_d(u, modes, False)),
        (5, 8, pointwise),
        (at_p, 1, lambda _: spectrum(0)),
        (at_p + CHUNKS, 1, lambda _: spectrum(1)),
        (at_q, UNITS, lambda u: inv.stage_q(u, False)),
        (at_t, UNITS, inv.stage_t),
        (at_r, UNITS, lambda u: inv.stage_r(u, False)),
        (at_s, CHUNKS, slope),
        (at_s, UNITS, fwd.send_a),
        (at_s + at_b, UNITS, lambda u: fwd.stage_b(u, True)),
        (at_s + at_e, UNITS, lambda u: fwd.stage_e(u, True)),
        (at_s + at_c, UNITS, lambda u: fwd.stage_c(u, True)),
        (at_s + at_d, UNITS, lambda u: fwd.stage_d(u, scaled, True)),
        (at_s + 5, 8, pointwise_back),
        (at_s + at_p, 1, lambda _: back_spectrum(0)),
        (at_s + at_p + CHUNKS, 1, lambda _: back_spectrum(1)),
        (at_s + at_q, UNITS, lambda u: inv.stage_q(u, True)),
        (at_s + at_t, UNITS, inv.stage_t),
        (at_s + at_r, UNITS, lambda u: inv.stage_r(u, True)),
        (at_s + 13, 1, across_columns),
        (at_s + 15, 1, across_rows),
        (at_s + at_s, CHUNKS, result),
    ])

    wait_for(row, small.at[3])
    total = row[0]
    for source in range(1, GY):
        total = total + row[source]
    total = total * (1.0 / math.sqrt(NX * NY * NZT))
    mixer_out[...] = total[:C, :C]
    bias_out[...] = total[C : C + 1, :C]
    wait_for(col.at[pl.ds(0, GX - 1)], small.at[0])
    wait_for(row.at[pl.ds(0, GY - 1)], small.at[2])

    @pl.loop(0, CHUNKS)
    def _(c):
        wait_for(gbuf.at[c], gsem.at[c])

    inv.finish()
    fwd.finish()


ANY = pl.BlockSpec(memory_space=pl.ANY)
VM = pl.BlockSpec(memory_space=pltpu.VMEM)


def params(number):
    return pltpu.CompilerParams(
        collective_id=number, has_side_effects=True, vmem_limit_bytes=60 * 2**20
    )


def body(layer_input, cotangent, spectral_weight, mixer_weight, bias_vector):
    depth, back, yf, yi, xf, xi = (jnp.asarray(v) for v in tables())
    grid = jnp.swapaxes(layer_input, 1, 2).reshape(XL, ROWS, NZT)
    cot = jnp.swapaxes(cotangent, 1, 2).reshape(XL, ROWS, NZT)
    weight = spectral_weight.reshape(8 * C, C, 2, 2, 128)
    weight = jnp.swapaxes(weight, 2, 3).reshape(8 * C, 4 * C, 128)
    modes_shape = jax.ShapeDtypeStruct((UNITS, 8, 8, 128), F32)
    chunked = pltpu.VMEM((CHUNKS, XL, CR, NZT), BF)
    chunk_sems = pltpu.SemaphoreType.DMA((CHUNKS,))
    flat = pltpu.VMEM((4 * C, 128), F32)

    input_grad, modes, scaled, mixer_grad, bias_grad = pl.pallas_call(
        whole_kernel,
        out_shape=[
            jax.ShapeDtypeStruct((XL, ROWS, NZT), BF),
            modes_shape,
            modes_shape,
            jax.ShapeDtypeStruct((C, C), F32),
            jax.ShapeDtypeStruct((1, C), F32),
        ],
        in_specs=[ANY, ANY, ANY, VM, VM] + [ANY] * 6,
        out_specs=[ANY, VM, VM, VM, VM],
        scratch_shapes=[
            chunked,
            chunked,
            pltpu.VMEM((XL, ROWS, NZT), F32),
            pltpu.VMEM((8 * C, 4 * C, 128), BF),
            flat,
            pltpu.VMEM((2, 8 * C, 128), F32),
            pltpu.VMEM((CHUNKS, 8, 8, 128), F32),
            pltpu.VMEM((32, KZT), F32),
            pltpu.VMEM((ROWS + 8, ROWS), F32),
            pltpu.VMEM((24, 128), F32),
            pltpu.VMEM((GX, 24, 128), F32),
            pltpu.VMEM((24, 128), F32),
            pltpu.VMEM((GY, 24, 128), F32),
            chunk_sems,
            chunk_sems,
            pltpu.SemaphoreType.DMA,
            pltpu.SemaphoreType.DMA((4,)),
        ]
        + FORWARD_TABLES
        + INVERSE_TABLES
        + INVERSE_SCRATCH
        + FORWARD_SCRATCH,
        compiler_params=params(1),
        name="whole",
    )(grid, cot, weight, mixer_weight, bias_vector.reshape(1, C), depth, yf, xf, back, yi, xi)

    field_spec = pl.BlockSpec((XL // 8, ROWS, NZT), lambda kl: (kl, 0, 0))
    modes_spec = pl.BlockSpec((UNITS, 8, 8, 128), lambda kl: (0, 0, 0, 0))
    spectral_grad, input_grad, mixer_grad, bias_grad = pl.pallas_call(
        gradient_kernel,
        out_shape=[
            jax.ShapeDtypeStruct((8 * C, 4 * C, 128), F32),
            jax.ShapeDtypeStruct((XL, ROWS, NZT), BF),
            jax.ShapeDtypeStruct((C, C), F32),
            jax.ShapeDtypeStruct((1, C), F32),
        ],
        grid=(8,),
        in_specs=[modes_spec, modes_spec, field_spec, VM, VM],
        out_specs=[pl.BlockSpec((C, 4 * C, 128), lambda kl: (kl, 0, 0)), field_spec, VM, VM],
        scratch_shapes=[flat],
        name="gradient",
    )(modes, scaled, input_grad, mixer_grad, bias_grad)
    spectral_grad = jnp.swapaxes(spectral_grad.reshape(8 * C, C, 2, 2, 128), 2, 3)
    spectral_grad = spectral_grad.reshape(4, 2, C, C, 2, KZT)
    input_grad = jnp.swapaxes(input_grad.reshape(XL, C, YL, NZT), 1, 2)
    return (input_grad, spectral_grad, mixer_grad, bias_grad.reshape(C))


def solution(mesh):
    return jax.shard_map(
        body,
        mesh=mesh,
        in_specs=(
            P("gx", "gy", None, None),
            P("gx", "gy", None, None),
            P("gx", "gy", None, None, None, None),
            P(),
            P(),
        ),
        out_specs=(P("gx", "gy", None, None), P("gx", "gy", None, None, None, None), P(), P()),
        check_vma=False,
    )
```

```python
import functools
import math

import jax
import jax.numpy as jnp
import ml_dtypes
import numpy as np
from jax import lax
from jax.experimental import pallas as pl
from jax.experimental.pallas import tpu as pltpu
from jax.sharding import PartitionSpec as P

NX = 128
NY = 128
NZ = 64
NT = 16
C = 20
MZ = 16
MT = 8
KX = 32
KY = 32
KZT = 256
NZT = 1024
GX = 8
GY = 16
HALF = 8
XL = NX // GX
YL = NY // GY
CHUNKS = 5
CC = C // CHUNKS
ROWS = C * YL
CR = CC * YL
BF = jnp.bfloat16
F32 = jnp.float32
MESH = pl.DeviceIdType.MESH


def signed_frequency(number):
    values = np.arange(number)
    return np.where(values < number // 2, values, values - number)


def pair_table(frequency, length):
    places = np.arange(length)
    phases = np.mod(frequency[:, None] * places[None, :], length)
    angles = phases * (-2.0 * math.pi / length)
    factor = float(length) ** (-0.5)
    cosine = np.cos(angles) * factor
    sine_part = np.sin(angles) * factor
    top_rows = np.stack([cosine, -sine_part], -1)
    low_rows = np.stack([sine_part, cosine], -1)
    return np.stack([top_rows, low_rows], 1)


def depth_table():
    fz = signed_frequency(2 * MZ)
    ft = np.arange(MT)
    z = np.arange(NZ)
    t = np.arange(NT)
    phases = (
        z[:, None, None, None] * fz[None, None, :, None] * NT
        + t[None, :, None, None] * ft[None, None, None, :] * NZ
    )
    phases = np.mod(phases, NZT).reshape(NZT, KZT)
    angles = phases * (-2.0 * math.pi / NZT)
    factor = float(NZT) ** (-0.5)
    stacked = np.stack([np.cos(angles) * factor, np.sin(angles) * factor], 1)
    return stacked.reshape(NZT, 2 * KZT)


def as_bf16(table):
    return np.ascontiguousarray(table).astype(np.float32).astype(ml_dtypes.bfloat16)


@functools.lru_cache(maxsize=None)
def tables():
    depth = depth_table()
    by_half = np.moveaxis(depth.reshape(NZT, 2, 2, 128), 2, 0).reshape(2, NZT, 256)
    xt = pair_table(signed_frequency(KX), NX)
    yt = pair_table(signed_frequency(KY), NY)
    eye = np.eye(2)
    yv = yt.reshape(GY, 2, 2, 2, HALF, YL, 2)
    yf = np.einsum("jlphsyq,cd,ab->hjalcpsbdqy", yv, eye, eye).reshape(2, 256, 512)
    xv = xt.reshape(GX, 4, 2, GX, HALF, 2, 2)
    xf = np.einsum("iapgsxq,cd,lm->gialcpsxmdq", xv, eye, eye).reshape(GX, 256, 128)
    yi = np.transpose(yf, (0, 2, 1))
    xi = np.transpose(xf, (0, 2, 1))
    return tuple(as_bf16(v) for v in (by_half, depth.T, yf, yi, xf, xi))


def mode_weight(shape):
    lanes = lax.broadcasted_iota(jnp.int32, shape, len(shape) - 1)
    return jnp.where(lax.rem(lanes, MT) == 0, 1.0, 2.0).astype(F32)


def gelu_slope(values):
    normal_cdf = 0.5 * (1.0 + lax.erf(values * (1.0 / math.sqrt(2.0))))
    density = jnp.exp(-0.5 * values * values) * (1.0 / math.sqrt(2.0 * math.pi))
    return normal_cdf + values * density


def mm(a, b):
    return jnp.dot(a, b, preferred_element_type=F32)


class Place:
    def __init__(self):
        self.gx = lax.axis_index("gx")
        self.gy = lax.axis_index("gy")
        self.lo = lax.rem(self.gy, HALF)
        self.hi = lax.div(self.gy, HALF)

    def x_peer(self, d):
        return lax.rem(self.gx + d, GX)

    def y_peer(self, d):
        return lax.rem(self.gy + d, GY)

    def half_peer(self, d):
        return lax.rem(self.lo + d, HALF)

    def greet(self):
        barrier = pltpu.get_barrier_semaphore()
        for d in range(1, GX):
            pl.semaphore_signal(
                barrier, inc=1, device_id={"gx": self.x_peer(d)}, device_id_type=MESH
            )
        for d in range(1, GY):
            pl.semaphore_signal(
                barrier, inc=1, device_id={"gy": self.y_peer(d)}, device_id_type=MESH
            )
        pl.semaphore_wait(barrier, GX + GY - 2)


def remote(src, dst, send, recv, device):
    pltpu.make_async_remote_copy(
        src_ref=src, dst_ref=dst, send_sem=send, recv_sem=recv,
        device_id=device, device_id_type=MESH,
    ).start()


def local(src, dst, sem):
    pltpu.make_async_copy(src, dst, sem).start()


def wait_for(region, sem):
    pltpu.make_async_copy(region, region, sem).wait()


def half_exchange(me, src, dst, send, recv):
    for d in range(1, HALF):
        peer = me.half_peer(d)
        remote(src.at[peer], dst.at[me.lo], send, recv, {"gy": me.hi * HALF + peer})
    local(src.at[me.lo], dst.at[me.lo], recv)


def twin(me, src, dst, send, recv):
    remote(src, dst, send, recv, {"gy": (1 - me.hi) * HALF + me.lo})


def column_exchange(me, src, dst, send, recv):
    for d in range(1, GX):
        peer = me.x_peer(d)
        remote(src.at[peer], dst.at[me.gx], send, recv, {"gx": peer})
    local(src.at[me.gx], dst.at[me.gx], recv)


def column_spread(me, src, dst, send, recv):
    for d in range(1, GX):
        remote(src, dst.at[me.gx], send, recv, {"gx": me.x_peer(d)})
    local(src, dst.at[me.gx], recv)


UNITS = 2 * CHUNKS
SLACK = (2, 2, 2, 2, 2, 2, 2, 2)
FORWARD_SCRATCH = [
    pltpu.VMEM((UNITS, HALF, 64, KZT), BF),
    pltpu.VMEM((UNITS, HALF, 64, KZT), BF),
    pltpu.VMEM((UNITS, 2, HALF, 16, KZT), BF),
    pltpu.VMEM((UNITS, HALF, 16, KZT), BF),
    pltpu.VMEM((UNITS, HALF, 16, KZT), BF),
    pltpu.VMEM((UNITS, HALF, 16, KZT), BF),
    pltpu.VMEM((UNITS, GX, 32, KZT), BF),
    pltpu.VMEM((UNITS, GX, 32, KZT), BF),
    pltpu.SemaphoreType.DMA((4, UNITS)),
    pltpu.SemaphoreType.DMA((4, UNITS)),
]
INVERSE_SCRATCH = [
    pltpu.VMEM((UNITS, 32, KZT), BF),
    pltpu.VMEM((UNITS, GX, 32, KZT), BF),
    pltpu.VMEM((UNITS, HALF, 16, KZT), BF),
    pltpu.VMEM((UNITS, 2, HALF, 16, KZT), BF),
    pltpu.VMEM((UNITS, HALF, 64, KZT), BF),
    pltpu.VMEM((UNITS, HALF, 64, KZT), BF),
    pltpu.SemaphoreType.DMA((4, UNITS)),
    pltpu.SemaphoreType.DMA((4, UNITS)),
]


class Forward:
    def __init__(self, me, depth, yf, xf, sa, ra, half, other, sb, rb, sc, rc, send, recv):
        self.me, self.depth, self.yf, self.xf = me, depth, yf, xf
        self.sa, self.ra, self.sb, self.rb, self.sc, self.rc = sa, ra, sb, rb, sc, rc
        self.half, self.other = half, other
        self.send, self.recv = send, recv

    def sent_a(self, u):
        wait_for(self.sa.at[u, pl.ds(0, HALF - 1)], self.send.at[0, u])

    def sent_b(self, u):
        wait_for(self.other.at[u], self.send.at[1, u])

    def sent_e(self, u):
        wait_for(self.sb.at[u, pl.ds(0, HALF - 1)], self.send.at[2, u])

    def sent_c(self, u):
        wait_for(self.sc.at[u, pl.ds(0, GX - 1)], self.send.at[3, u])

    def put(self, u, table, part, parts, grid):
        count = XL // parts
        modes = mm(grid, table)
        real = modes[:, :128].reshape(count, 2, 2, 1, YL, 128)
        imag = modes[:, 128:].reshape(count, 2, 2, 1, YL, 128)
        both = jnp.concatenate([real, imag], 3)
        both = jnp.concatenate([both[:, 0], both[:, 1]], -1).reshape(count * 32, KZT)
        self.sa[u, pl.ds(part * (count // 2), count // 2)] = both.astype(BF).reshape(
            count // 2, 64, KZT
        )

    def send_a(self, u):
        half_exchange(
            self.me, self.sa.at[u], self.ra.at[u], self.send.at[0, u], self.recv.at[0, u]
        )

    def stage_b(self, u, again):
        wait_for(self.ra.at[u], self.recv.at[0, u])
        if again:
            self.sent_b(u)
        block = self.ra[u].reshape(512, KZT)
        self.half[u] = mm(self.yf[...], block).astype(BF).reshape(2, HALF, 16, KZT)
        twin(
            self.me, self.half.at[u, 1 - self.me.hi], self.other.at[u],
            self.send.at[1, u], self.recv.at[1, u],
        )

    def stage_e(self, u, again):
        wait_for(self.other.at[u], self.recv.at[1, u])
        if again:
            self.sent_e(u)
        mine = self.half[u, pl.ds(self.me.hi, 1)].reshape(HALF, 16, KZT)
        self.sb[u] = (mine.astype(F32) + self.other[u].astype(F32)).astype(BF)
        half_exchange(
            self.me, self.sb.at[u], self.rb.at[u], self.send.at[2, u], self.recv.at[2, u]
        )

    def stage_c(self, u, again):
        wait_for(self.rb.at[u], self.recv.at[2, u])
        if again:
            self.sent_c(u)
        block = self.rb[u].reshape(128, KZT)
        self.sc[u] = mm(self.xf[...], block).astype(BF).reshape(GX, 32, KZT)
        column_exchange(
            self.me, self.sc.at[u], self.rc.at[u], self.send.at[3, u], self.recv.at[3, u]
        )

    def stage_d(self, u, out, weighted):
        wait_for(self.rc.at[u], self.recv.at[3, u])
        total = self.rc[u, 0].astype(F32)
        for source in range(1, GX):
            total = total + self.rc[u, source].astype(F32)
        if weighted:
            total = total * mode_weight(total.shape)
        for kl in range(8):
            for pair in range(2):
                out[u, kl, pair * 4 : pair * 4 + 4, :] = total[
                    kl * 4 : kl * 4 + 4, pair * 128 : pair * 128 + 128
                ]

    def finish(self):
        @pl.loop(0, UNITS)
        def _(u):
            self.sent_a(u)
            self.sent_b(u)
            self.sent_e(u)
            self.sent_c(u)


class Inverse:
    def __init__(self, me, back, yi, xi, spec, rp, sq, rq, sr, rr, send, recv):
        self.me, self.back, self.yi, self.xi, self.spec = me, back, yi, xi, spec
        self.rp, self.sq, self.rq, self.sr, self.rr = rp, sq, rq, sr, rr
        self.send, self.recv = send, recv

    def sent_p(self, u):
        wait_for(self.rp.at[u, pl.ds(0, GX - 1)], self.send.at[0, u])

    def sent_q(self, u):
        wait_for(self.sq.at[u, pl.ds(0, HALF - 1)], self.send.at[1, u])

    def sent_r(self, u):
        wait_for(self.sr.at[u, pl.ds(0, HALF - 1)], self.send.at[3, u])

    def start(self, half, spec, unit, again):
        for c in range(CHUNKS):
            u = half * CHUNKS + c
            for kl in range(8):
                for pair in range(2):
                    unit[kl * 4 : kl * 4 + 4, pair * 128 : pair * 128 + 128] = spec[
                        c, kl, pair * 4 : pair * 4 + 4, :
                    ]
            if again:
                self.sent_p(u)
            self.spec[u] = unit[...].astype(BF)

        @pl.loop(half * CHUNKS, half * CHUNKS + CHUNKS)
        def _(u):
            column_spread(
                self.me, self.spec.at[u], self.rp.at[u], self.send.at[0, u], self.recv.at[0, u]
            )

    def stage_q(self, u, again):
        wait_for(self.rp.at[u], self.recv.at[0, u])
        if again:
            self.sent_q(u)
        block = self.rp[u].reshape(256, KZT)
        self.sq[u] = mm(self.xi[...], block).astype(BF).reshape(HALF, 16, KZT)
        half_exchange(
            self.me, self.sq.at[u], self.rq.at[u, self.me.hi],
            self.send.at[1, u], self.recv.at[1, u],
        )

    def stage_t(self, u):
        mine = self.rq.at[u, self.me.hi]
        wait_for(mine, self.recv.at[1, u])
        twin(self.me, mine, mine, self.send.at[2, u], self.recv.at[2, u])

    def stage_r(self, u, again):
        wait_for(self.rq.at[u, 1 - self.me.hi], self.recv.at[2, u])
        wait_for(self.sq.at[u], self.send.at[2, u])
        if again:
            self.sent_r(u)
        block = self.rq[u].reshape(256, KZT)
        self.sr[u] = mm(self.yi[...], block).astype(BF).reshape(HALF, 64, KZT)
        half_exchange(
            self.me, self.sr.at[u], self.rr.at[u], self.send.at[3, u], self.recv.at[3, u]
        )

    def ready(self, c):
        for half in range(2):
            u = half * CHUNKS + c
            wait_for(self.rr.at[u], self.recv.at[3, u])

    def branch(self, c, part, parts):
        count = XL // parts
        total = None
        for p in range(2):
            halves = []
            for half in range(2):
                block = self.rr[half * CHUNKS + c, pl.ds(part * (count // 2), count // 2)]
                block = block.astype(F32).reshape(count, 2, 2, YL, KZT)[:, :, p]
                block = [block[:, None, :, :, :128], block[:, None, :, :, 128:]]
                halves.append(jnp.concatenate(block, 1))
            lhs = jnp.concatenate(halves, -1).reshape(count * CR, KZT).astype(BF)
            term = mm(lhs, self.back[p * KZT : p * KZT + KZT, :])
            total = term if total is None else total + term
        return total

    def finish(self):
        @pl.loop(0, UNITS)
        def _(u):
            self.sent_p(u)
            self.sent_q(u)
            self.sent_r(u)


def run(schedule):
    steps = max(start + count for start, count, _ in schedule)

    @pl.loop(0, steps)
    def _(t):
        for start, count, stage in schedule:
            @pl.when(jnp.logical_and(t >= start, t < start + count))
            def _(stage=stage, start=start):
                stage(t - start)


TILES = 10
TILE = (TILES, 8, 128)


def swap_parts(tiles):
    even = (lax.rem(lax.broadcasted_iota(jnp.int32, TILE, 1), 2) == 0)
    return jnp.where(even, pltpu.roll(tiles, 7, 1), pltpu.roll(tiles, 1, 1)), even


def coefficient(modes, half, kl, i, part):
    row = pl.ds((i % CC) * 2 + part, 1)
    return jnp.broadcast_to(modes[half * CHUNKS + i // CC, kl, row, :], (8, 128))


def lay_out(modes, half, kl, flat):
    for c in range(CHUNKS):
        for part in range(2):
            flat[pl.ds(c * 16 + half * 2 + part, CC, 4), :] = modes[
                half * CHUNKS + c, kl, pl.ds(part, CC, 2), :
            ]


def mix_modes(modes, half, weight, flat, spec):
    @pl.loop(0, 8)
    def _(kl):
        by_real = jnp.zeros(TILE, F32)
        by_imag = jnp.zeros(TILE, F32)
        for i in range(C):
            block = weight[kl * C + i].astype(F32).reshape(TILE)
            by_real = by_real + block * coefficient(modes, half, kl, i, 0)[None]
            by_imag = by_imag + block * coefficient(modes, half, kl, i, 1)[None]
        turned, even = swap_parts(by_imag)
        mixed = by_real + jnp.where(even, -turned, turned)
        flat[...] = (mixed * mode_weight(TILE)).reshape(80, 128)
        for c in range(CHUNKS):
            for part in range(2):
                spec[c, kl, pl.ds(part, CC, 2), :] = flat[
                    pl.ds(c * 16 + half * 2 + part, CC, 4), :
                ]


def adjoint_modes(scaled, half, weight, flat, sums, spec):
    @pl.loop(0, 8)
    def _(kl):
        lay_out(scaled, half, kl, flat)
        grad = flat[...].reshape(TILE)
        turned, even = swap_parts(grad)
        turned = jnp.where(even, turned, -turned)
        for i in range(C):
            block = weight[kl * C + i].astype(F32).reshape(TILE)
            sums[0, i * 8 : i * 8 + 8] = (block * grad).sum(0)
            sums[1, i * 8 : i * 8 + 8] = (block * turned).sum(0)
        for c in range(CHUNKS):
            for part in range(2):
                total = None
                for row in (0, 1, 4, 5):
                    term = sums[part, pl.ds(c * 32 + half * 2 + row, CC, 8), :]
                    total = term if total is None else total + term
                spec[c, kl, pl.ds(part, CC, 2), :] = total


def gradient_kernel(modes, scaled, field, mixer, bias, out, field_out, mixer_out, bias_out, flat):
    field_out[...] = field[...]
    mixer_out[...] = mixer[...]
    bias_out[...] = bias[...]
    kl = pl.program_id(0)
    for half in range(2):
        lay_out(scaled, half, kl, flat)
    grad = flat[...].reshape(TILE)
    turned, even = swap_parts(grad)
    turned = jnp.where(even, turned, -turned)
    first = lax.rem(lax.broadcasted_iota(jnp.int32, (8, 128), 0), 4) < 2
    for i in range(C):
        real, imag = (
            jnp.where(first, coefficient(modes, 0, kl, i, p), coefficient(modes, 1, kl, i, p))
            for p in range(2)
        )
        out[i] = (grad * real[None] + turned * imag[None]).reshape(80, 128)


def channel_rows():
    rows = lax.broadcasted_iota(jnp.int32, (ROWS, C), 0)
    return lax.div(rows, YL) == lax.broadcasted_iota(jnp.int32, (ROWS, C), 1)


def same_place():
    rows = lax.broadcasted_iota(jnp.int32, (ROWS, ROWS), 0)
    columns = lax.broadcasted_iota(jnp.int32, (ROWS, ROWS), 1)
    return lax.rem(rows, YL) == lax.rem(columns, YL)


def spread_mixer(mixer, axis):
    spread = jnp.where(channel_rows(), 1.0, 0.0).astype(BF)
    half = lax.dot_general(
        spread, mixer, (((1,), (1 - axis,)), ((), ())), preferred_element_type=F32
    ).astype(BF)
    full = lax.dot_general(
        half, spread, (((1,), (1,)), ((), ())), preferred_element_type=F32
    )
    return jnp.where(same_place(), full, 0.0).astype(BF)


FORWARD_TABLES = [
    pltpu.VMEM((2, NZT, KZT), BF),
    pltpu.VMEM((256, 512), BF),
    pltpu.VMEM((256, 128), BF),
    pltpu.SemaphoreType.DMA((3,)),
]
INVERSE_TABLES = [
    pltpu.VMEM((2 * KZT, NZT), BF),
    pltpu.VMEM((512, 256), BF),
    pltpu.VMEM((128, 256), BF),
    pltpu.SemaphoreType.DMA((3,)),
]


def fetch_tables(me, depth_hbm, y_hbm, x_hbm, depth, y, x, sem):
    pairs = ((depth_hbm, depth), (y_hbm.at[me.hi], y), (x_hbm.at[me.gx], x))
    for n, (src, dst) in enumerate(pairs):
        local(src, dst, sem.at[n])

    def ready():
        for n, (_, dst) in enumerate(pairs):
            wait_for(dst, sem.at[n])

    return ready


def whole_kernel(
    x_hbm, cot_hbm, weight_hbm, mixer, bias, depth_hbm, yf_hbm, xf_hbm, back_hbm, yi_hbm, xi_hbm,
    out_hbm, modes, scaled, mixer_out, bias_out,
    gbuf, cbuf, point, weight, flat, sums, spec, unit, mixed, one, col, two, row,
    gsem, csem, wsem, small, *scratch
):
    me = Place()
    n = len(FORWARD_TABLES)
    depth, yf, xf, tsem, back, yi, xi, isem = scratch[: 2 * n]
    scratch = scratch[2 * n :]

    def chunk_of(ref, c):
        return ref.at[:, pl.ds(c * CR, CR), :]

    local(chunk_of(x_hbm, 0), gbuf.at[0], gsem.at[0])
    forward_ready = fetch_tables(me, depth_hbm, yf_hbm, xf_hbm, depth, yf, xf, tsem)

    @pl.loop(1, CHUNKS)
    def _(c):
        local(chunk_of(x_hbm, c), gbuf.at[c], gsem.at[c])

    local(weight_hbm, weight, wsem)
    inverse_ready = fetch_tables(me, back_hbm, yi_hbm, xi_hbm, back, yi, xi, isem)

    @pl.loop(0, CHUNKS)
    def _(c):
        local(chunk_of(cot_hbm, c), cbuf.at[c], csem.at[c])

    me.greet()
    n = len(INVERSE_SCRATCH)
    inv = Inverse(me, back, yi, xi, *scratch[:n])
    fwd = Forward(me, depth, yf, xf, *scratch[n:])
    flat[...] = jnp.zeros_like(flat)
    mixed[...] = jnp.zeros_like(mixed)
    forward_ready()

    def first_a(u):
        c = lax.rem(u, CHUNKS)

        @pl.when(u < CHUNKS)
        def _():
            wait_for(gbuf.at[c], gsem.at[c])

        table = depth[lax.div(u, CHUNKS)]
        for part in range(2):
            fwd.put(u, table, part, 2, gbuf[c, part * 8 : part * 8 + 8].reshape(8 * CR, NZT))
        fwd.send_a(u)

    def spectrum(half):
        if half == 0:
            wait_for(weight, wsem)
            inverse_ready()
        mix_modes(modes, half, weight, flat, spec)
        inv.start(half, spec, unit, False)

    def back_spectrum(half):
        adjoint_modes(scaled, half, weight, flat, sums, spec)
        inv.start(half, spec, unit, True)

    def pointwise(n):
        spread = spread_mixer(mixer[...], 0)
        shift = jnp.where(channel_rows(), bias[...], 0.0).sum(1, keepdims=True)
        for x in (2 * n, 2 * n + 1):
            point[x] = mm(spread, gbuf[:, x].reshape(ROWS, NZT)) + shift

    def slope(c):
        inv.ready(c)
        wait_for(cbuf.at[c], csem.at[c])
        fwd.sent_a(c)
        fwd.sent_a(CHUNKS + c)

        @pl.loop(0, 2)
        def _(part):
            rows = pl.ds(part * 8, 8)
            pre = inv.branch(c, part, 2)
            pre = pre + point[rows, pl.ds(c * CR, CR), :].reshape(8 * CR, NZT)
            cot = cbuf[c, rows].reshape(8 * CR, NZT).astype(F32)
            grad = (cot * gelu_slope(pre)).astype(BF)
            gbuf[c, rows] = grad.reshape(8, CR, NZT)
            for half in range(2):
                fwd.put(half * CHUNKS + c, depth[half], part, 2, grad)

        local(chunk_of(x_hbm, c), cbuf.at[c], csem.at[c])

    def pointwise_back(n):
        @pl.when(n == 0)
        def _():
            @pl.loop(0, CHUNKS)
            def _(c):
                wait_for(cbuf.at[c], csem.at[c])

        spread = spread_mixer(mixer[...], 1)
        contract = (((1,), (1,)), ((), ()))
        for x in (2 * n, 2 * n + 1):
            grad = gbuf[:, x].reshape(ROWS, NZT)
            point[x] = mm(spread, grad)
            mixed[:ROWS, :] += lax.dot_general(
                cbuf[:, x].reshape(ROWS, NZT), grad, contract, preferred_element_type=F32
            )
            mixed[ROWS:, :] += lax.dot_general(
                jnp.ones((8, NZT), BF), grad, contract, preferred_element_type=F32
            )

    def across_columns(_):
        kept = jnp.where(same_place(), mixed[:ROWS, :], 0.0).reshape(C, YL, ROWS).sum(1)
        stacked = jnp.concatenate([kept, mixed[ROWS : ROWS + 4, :]], 0)
        fold = lax.div(lax.broadcasted_iota(jnp.int32, (ROWS, 128), 0), YL)
        fold = fold == lax.broadcasted_iota(jnp.int32, (ROWS, 128), 1)
        one[...] = lax.dot_general(
            stacked, jnp.where(fold, 1.0, 0.0), (((1,), (0,)), ((), ())),
            precision=lax.Precision.HIGHEST, preferred_element_type=F32,
        )
        for d in range(1, GX):
            remote(one, col.at[me.gx], small.at[0], small.at[1], {"gx": me.x_peer(d)})
        local(one, col.at[me.gx], small.at[1])

    def across_rows(_):
        wait_for(col, small.at[1])
        total = col[0]
        for source in range(1, GX):
            total = total + col[source]
        two[...] = total
        for d in range(1, GY):
            remote(two, row.at[me.gy], small.at[2], small.at[3], {"gy": me.y_peer(d)})
        local(two, row.at[me.gy], small.at[3])

    def result(c):
        inv.ready(c)

        @pl.loop(0, 2)
        def _(part):
            rows = pl.ds(part * 8, 8)
            total = inv.branch(c, part, 2)
            total = total + point[rows, pl.ds(c * CR, CR), :].reshape(8 * CR, NZT)
            gbuf[c, rows] = total.astype(BF).reshape(8, CR, NZT)

        local(gbuf.at[c], chunk_of(out_hbm, c), gsem.at[c])

    send_b, send_e, send_c, send_d, send_q, send_t, send_r, send_s = SLACK
    at_b = send_b
    at_e = at_b + send_e
    at_c = at_e + send_c
    at_d = at_c + send_d
    at_p = at_d + CHUNKS - 1
    at_q = at_p + send_q
    at_t = at_q + send_t
    at_r = at_t + send_r
    at_s = at_r + CHUNKS + send_s
    run([
        (at_e, UNITS, lambda u: fwd.stage_e(u, False)),
        (at_s + at_e, UNITS, lambda u: fwd.stage_e(u, True)),
        (at_c, UNITS, lambda u: fwd.stage_c(u, False)),
        (at_s + at_c, UNITS, lambda u: fwd.stage_c(u, True)),
        (at_d, UNITS, lambda u: fwd.stage_d(u, modes, False)),
        (at_s + at_d, UNITS, lambda u: fwd.stage_d(u, scaled, True)),
        (at_q, UNITS, lambda u: inv.stage_q(u, False)),
        (at_s + at_q, UNITS, lambda u: inv.stage_q(u, True)),
        (at_t, UNITS, inv.stage_t),
        (at_s + at_t, UNITS, inv.stage_t),
        (at_b, UNITS, lambda u: fwd.stage_b(u, False)),
        (at_s + at_b, UNITS, lambda u: fwd.stage_b(u, True)),
        (at_r, UNITS, lambda u: inv.stage_r(u, False)),
        (at_s + at_r, UNITS, lambda u: inv.stage_r(u, True)),
        (0, UNITS, first_a),
        (at_s, CHUNKS, slope),
        (at_s, UNITS, fwd.send_a),
        (5, 8, pointwise),
        (at_p, 1, lambda _: spectrum(0)),
        (at_p + CHUNKS, 1, lambda _: spectrum(1)),
        (at_s + at_p, 1, lambda _: back_spectrum(0)),
        (at_s + at_p + CHUNKS, 1, lambda _: back_spectrum(1)),
        (at_s + 5, 8, pointwise_back),
        (at_s + 13, 1, across_columns),
        (at_s + 15, 1, across_rows),
        (at_s + at_s, CHUNKS, result),
    ])

    wait_for(row, small.at[3])
    total = row[0]
    for source in range(1, GY):
        total = total + row[source]
    total = total * (1.0 / math.sqrt(NX * NY * NZT))
    mixer_out[...] = total[:C, :C]
    bias_out[...] = total[C : C + 1, :C]
    wait_for(col.at[pl.ds(0, GX - 1)], small.at[0])
    wait_for(row.at[pl.ds(0, GY - 1)], small.at[2])

    @pl.loop(0, CHUNKS)
    def _(c):
        wait_for(gbuf.at[c], gsem.at[c])

    inv.finish()
    fwd.finish()


ANY = pl.BlockSpec(memory_space=pl.ANY)
VM = pl.BlockSpec(memory_space=pltpu.VMEM)


def params(number):
    return pltpu.CompilerParams(
        collective_id=number, has_side_effects=True, vmem_limit_bytes=60 * 2**20
    )


def body(layer_input, cotangent, spectral_weight, mixer_weight, bias_vector):
    depth, back, yf, yi, xf, xi = (jnp.asarray(v) for v in tables())
    grid = jnp.swapaxes(layer_input, 1, 2).reshape(XL, ROWS, NZT)
    cot = jnp.swapaxes(cotangent, 1, 2).reshape(XL, ROWS, NZT)
    weight = spectral_weight.reshape(8 * C, C, 2, 2, 128)
    weight = jnp.swapaxes(weight, 2, 3).reshape(8 * C, 4 * C, 128)
    modes_shape = jax.ShapeDtypeStruct((UNITS, 8, 8, 128), F32)
    chunked = pltpu.VMEM((CHUNKS, XL, CR, NZT), BF)
    chunk_sems = pltpu.SemaphoreType.DMA((CHUNKS,))
    flat = pltpu.VMEM((4 * C, 128), F32)

    input_grad, modes, scaled, mixer_grad, bias_grad = pl.pallas_call(
        whole_kernel,
        out_shape=[
            jax.ShapeDtypeStruct((XL, ROWS, NZT), BF),
            modes_shape,
            modes_shape,
            jax.ShapeDtypeStruct((C, C), F32),
            jax.ShapeDtypeStruct((1, C), F32),
        ],
        in_specs=[ANY, ANY, ANY, VM, VM] + [ANY] * 6,
        out_specs=[ANY, VM, VM, VM, VM],
        scratch_shapes=[
            chunked,
            chunked,
            pltpu.VMEM((XL, ROWS, NZT), F32),
            pltpu.VMEM((8 * C, 4 * C, 128), BF),
            flat,
            pltpu.VMEM((2, 8 * C, 128), F32),
            pltpu.VMEM((CHUNKS, 8, 8, 128), F32),
            pltpu.VMEM((32, KZT), F32),
            pltpu.VMEM((ROWS + 8, ROWS), F32),
            pltpu.VMEM((24, 128), F32),
            pltpu.VMEM((GX, 24, 128), F32),
            pltpu.VMEM((24, 128), F32),
            pltpu.VMEM((GY, 24, 128), F32),
            chunk_sems,
            chunk_sems,
            pltpu.SemaphoreType.DMA,
            pltpu.SemaphoreType.DMA((4,)),
        ]
        + FORWARD_TABLES
        + INVERSE_TABLES
        + INVERSE_SCRATCH
        + FORWARD_SCRATCH,
        compiler_params=params(1),
        name="whole",
    )(grid, cot, weight, mixer_weight, bias_vector.reshape(1, C), depth, yf, xf, back, yi, xi)

    field_spec = pl.BlockSpec((XL // 8, ROWS, NZT), lambda kl: (kl, 0, 0))
    modes_spec = pl.BlockSpec((UNITS, 8, 8, 128), lambda kl: (0, 0, 0, 0))
    spectral_grad, input_grad, mixer_grad, bias_grad = pl.pallas_call(
        gradient_kernel,
        out_shape=[
            jax.ShapeDtypeStruct((8 * C, 4 * C, 128), F32),
            jax.ShapeDtypeStruct((XL, ROWS, NZT), BF),
            jax.ShapeDtypeStruct((C, C), F32),
            jax.ShapeDtypeStruct((1, C), F32),
        ],
        grid=(8,),
        in_specs=[modes_spec, modes_spec, field_spec, VM, VM],
        out_specs=[pl.BlockSpec((C, 4 * C, 128), lambda kl: (kl, 0, 0)), field_spec, VM, VM],
        scratch_shapes=[flat],
        name="gradient",
    )(modes, scaled, input_grad, mixer_grad, bias_grad)
    spectral_grad = jnp.swapaxes(spectral_grad.reshape(8 * C, C, 2, 2, 128), 2, 3)
    spectral_grad = spectral_grad.reshape(4, 2, C, C, 2, KZT)
    input_grad = jnp.swapaxes(input_grad.reshape(XL, C, YL, NZT), 1, 2)
    return (input_grad, spectral_grad, mixer_grad, bias_grad.reshape(C))


def solution(mesh):
    return jax.shard_map(
        body,
        mesh=mesh,
        in_specs=(
            P("gx", "gy", None, None),
            P("gx", "gy", None, None),
            P("gx", "gy", None, None, None, None),
            P(),
            P(),
        ),
        out_specs=(P("gx", "gy", None, None), P("gx", "gy", None, None, None, None), P(), P()),
        check_vma=False,
    )
```

```python
import functools
import math

import jax
import jax.numpy as jnp
import ml_dtypes
import numpy as np
from jax import lax
from jax.experimental import pallas as pl
from jax.experimental.pallas import tpu as pltpu
from jax.sharding import PartitionSpec as P

NX = 128
NY = 128
NZ = 64
NT = 16
C = 20
MZ = 16
MT = 8
KX = 32
KY = 32
KZT = 256
NZT = 1024
GX = 8
GY = 16
HALF = 8
XL = NX // GX
YL = NY // GY
CHUNKS = 5
CC = C // CHUNKS
ROWS = C * YL
CR = CC * YL
BF = jnp.bfloat16
F32 = jnp.float32
MESH = pl.DeviceIdType.MESH


def signed_frequency(number):
    values = np.arange(number)
    return np.where(values < number // 2, values, values - number)


def pair_table(frequency, length):
    places = np.arange(length)
    phases = np.mod(frequency[:, None] * places[None, :], length)
    angles = phases * (-2.0 * math.pi / length)
    factor = float(length) ** (-0.5)
    cosine = np.cos(angles) * factor
    sine_part = np.sin(angles) * factor
    top_rows = np.stack([cosine, -sine_part], -1)
    low_rows = np.stack([sine_part, cosine], -1)
    return np.stack([top_rows, low_rows], 1)


def depth_table():
    fz = signed_frequency(2 * MZ)
    ft = np.arange(MT)
    z = np.arange(NZ)
    t = np.arange(NT)
    phases = (
        z[:, None, None, None] * fz[None, None, :, None] * NT
        + t[None, :, None, None] * ft[None, None, None, :] * NZ
    )
    phases = np.mod(phases, NZT).reshape(NZT, KZT)
    angles = phases * (-2.0 * math.pi / NZT)
    factor = float(NZT) ** (-0.5)
    stacked = np.stack([np.cos(angles) * factor, np.sin(angles) * factor], 1)
    return stacked.reshape(NZT, 2 * KZT)


def as_bf16(table):
    return np.ascontiguousarray(table).astype(np.float32).astype(ml_dtypes.bfloat16)


@functools.lru_cache(maxsize=None)
def tables():
    depth = depth_table()
    by_half = np.moveaxis(depth.reshape(NZT, 2, 2, 128), 2, 0).reshape(2, NZT, 256)
    xt = pair_table(signed_frequency(KX), NX)
    yt = pair_table(signed_frequency(KY), NY)
    eye = np.eye(2)
    yv = yt.reshape(GY, 2, 2, 2, HALF, YL, 2)
    yf = np.einsum("jlphsyq,cd,ab->hjalcpsbdqy", yv, eye, eye).reshape(2, 256, 512)
    xv = xt.reshape(GX, 4, 2, GX, HALF, 2, 2)
    xf = np.einsum("iapgsxq,cd,lm->gialcpsxmdq", xv, eye, eye).reshape(GX, 256, 128)
    yi = np.transpose(yf, (0, 2, 1))
    xi = np.transpose(xf, (0, 2, 1))
    return tuple(as_bf16(v) for v in (by_half, depth.T, yf, yi, xf, xi))


def mode_weight(shape):
    lanes = lax.broadcasted_iota(jnp.int32, shape, len(shape) - 1)
    return jnp.where(lax.rem(lanes, MT) == 0, 1.0, 2.0).astype(F32)


def gelu_slope(values):
    normal_cdf = 0.5 * (1.0 + lax.erf(values * (1.0 / math.sqrt(2.0))))
    density = jnp.exp(-0.5 * values * values) * (1.0 / math.sqrt(2.0 * math.pi))
    return normal_cdf + values * density


def mm(a, b):
    return jnp.dot(a, b, preferred_element_type=F32)


class Place:
    def __init__(self):
        self.gx = lax.axis_index("gx")
        self.gy = lax.axis_index("gy")
        self.lo = lax.rem(self.gy, HALF)
        self.hi = lax.div(self.gy, HALF)

    def x_peer(self, d):
        return lax.rem(self.gx + d, GX)

    def y_peer(self, d):
        return lax.rem(self.gy + d, GY)

    def half_peer(self, d):
        return lax.rem(self.lo + d, HALF)

    def greet(self):
        barrier = pltpu.get_barrier_semaphore()
        for d in range(1, GX):
            pl.semaphore_signal(
                barrier, inc=1, device_id={"gx": self.x_peer(d)}, device_id_type=MESH
            )
        for d in range(1, GY):
            pl.semaphore_signal(
                barrier, inc=1, device_id={"gy": self.y_peer(d)}, device_id_type=MESH
            )
        pl.semaphore_wait(barrier, GX + GY - 2)


def remote(src, dst, send, recv, device):
    pltpu.make_async_remote_copy(
        src_ref=src, dst_ref=dst, send_sem=send, recv_sem=recv,
        device_id=device, device_id_type=MESH,
    ).start()


def local(src, dst, sem):
    pltpu.make_async_copy(src, dst, sem).start()


def wait_for(region, sem):
    pltpu.make_async_copy(region, region, sem).wait()


def half_exchange(me, src, dst, send, recv):
    for d in range(1, HALF):
        peer = me.half_peer(d)
        remote(src.at[peer], dst.at[me.lo], send, recv, {"gy": me.hi * HALF + peer})
    local(src.at[me.lo], dst.at[me.lo], recv)


def twin(me, src, dst, send, recv):
    remote(src, dst, send, recv, {"gy": (1 - me.hi) * HALF + me.lo})


def column_exchange(me, src, dst, send, recv):
    for d in range(1, GX):
        peer = me.x_peer(d)
        remote(src.at[peer], dst.at[me.gx], send, recv, {"gx": peer})
    local(src.at[me.gx], dst.at[me.gx], recv)


def column_spread(me, src, dst, send, recv):
    for d in range(1, GX):
        remote(src, dst.at[me.gx], send, recv, {"gx": me.x_peer(d)})
    local(src, dst.at[me.gx], recv)


UNITS = 2 * CHUNKS
SLACK = (2, 2, 3, 3, 2, 3, 3, 2)
FORWARD_SCRATCH = [
    pltpu.VMEM((UNITS, HALF, 64, KZT), BF),
    pltpu.VMEM((UNITS, HALF, 64, KZT), BF),
    pltpu.VMEM((UNITS, 2, HALF, 16, KZT), BF),
    pltpu.VMEM((UNITS, HALF, 16, KZT), BF),
    pltpu.VMEM((UNITS, HALF, 16, KZT), BF),
    pltpu.VMEM((UNITS, HALF, 16, KZT), BF),
    pltpu.VMEM((UNITS, GX, 32, KZT), BF),
    pltpu.VMEM((UNITS, GX, 32, KZT), BF),
    pltpu.SemaphoreType.DMA((4, UNITS)),
    pltpu.SemaphoreType.DMA((4, UNITS)),
]
INVERSE_SCRATCH = [
    pltpu.VMEM((UNITS, 32, KZT), BF),
    pltpu.VMEM((UNITS, GX, 32, KZT), BF),
    pltpu.VMEM((UNITS, HALF, 16, KZT), BF),
    pltpu.VMEM((UNITS, 2, HALF, 16, KZT), BF),
    pltpu.VMEM((UNITS, HALF, 64, KZT), BF),
    pltpu.VMEM((UNITS, HALF, 64, KZT), BF),
    pltpu.SemaphoreType.DMA((4, UNITS)),
    pltpu.SemaphoreType.DMA((4, UNITS)),
]


class Forward:
    def __init__(self, me, depth, yf, xf, sa, ra, half, other, sb, rb, sc, rc, send, recv):
        self.me, self.depth, self.yf, self.xf = me, depth, yf, xf
        self.sa, self.ra, self.sb, self.rb, self.sc, self.rc = sa, ra, sb, rb, sc, rc
        self.half, self.other = half, other
        self.send, self.recv = send, recv

    def sent_a(self, u):
        wait_for(self.sa.at[u, pl.ds(0, HALF - 1)], self.send.at[0, u])

    def sent_b(self, u):
        wait_for(self.other.at[u], self.send.at[1, u])

    def sent_e(self, u):
        wait_for(self.sb.at[u, pl.ds(0, HALF - 1)], self.send.at[2, u])

    def sent_c(self, u):
        wait_for(self.sc.at[u, pl.ds(0, GX - 1)], self.send.at[3, u])

    def put(self, u, table, part, parts, grid):
        count = XL // parts
        modes = mm(grid, table)
        real = modes[:, :128].reshape(count, 2, 2, 1, YL, 128)
        imag = modes[:, 128:].reshape(count, 2, 2, 1, YL, 128)
        both = jnp.concatenate([real, imag], 3)
        both = jnp.concatenate([both[:, 0], both[:, 1]], -1).reshape(count * 32, KZT)
        self.sa[u, pl.ds(part * (count // 2), count // 2)] = both.astype(BF).reshape(
            count // 2, 64, KZT
        )

    def send_a(self, u):
        half_exchange(
            self.me, self.sa.at[u], self.ra.at[u], self.send.at[0, u], self.recv.at[0, u]
        )

    def stage_b(self, u, again):
        wait_for(self.ra.at[u], self.recv.at[0, u])
        if again:
            self.sent_b(u)
        block = self.ra[u].reshape(512, KZT)
        self.half[u] = mm(self.yf[...], block).astype(BF).reshape(2, HALF, 16, KZT)
        twin(
            self.me, self.half.at[u, 1 - self.me.hi], self.other.at[u],
            self.send.at[1, u], self.recv.at[1, u],
        )

    def stage_e(self, u, again):
        wait_for(self.other.at[u], self.recv.at[1, u])
        if again:
            self.sent_e(u)
        mine = self.half[u, pl.ds(self.me.hi, 1)].reshape(HALF, 16, KZT)
        self.sb[u] = (mine.astype(F32) + self.other[u].astype(F32)).astype(BF)
        half_exchange(
            self.me, self.sb.at[u], self.rb.at[u], self.send.at[2, u], self.recv.at[2, u]
        )

    def stage_c(self, u, again):
        wait_for(self.rb.at[u], self.recv.at[2, u])
        if again:
            self.sent_c(u)
        block = self.rb[u].reshape(128, KZT)
        self.sc[u] = mm(self.xf[...], block).astype(BF).reshape(GX, 32, KZT)
        column_exchange(
            self.me, self.sc.at[u], self.rc.at[u], self.send.at[3, u], self.recv.at[3, u]
        )

    def stage_d(self, u, out, weighted):
        wait_for(self.rc.at[u], self.recv.at[3, u])
        total = self.rc[u, 0].astype(F32)
        for source in range(1, GX):
            total = total + self.rc[u, source].astype(F32)
        if weighted:
            total = total * mode_weight(total.shape)
        for kl in range(8):
            for pair in range(2):
                out[u, kl, pair * 4 : pair * 4 + 4, :] = total[
                    kl * 4 : kl * 4 + 4, pair * 128 : pair * 128 + 128
                ]

    def finish(self):
        @pl.loop(0, UNITS)
        def _(u):
            self.sent_a(u)
            self.sent_b(u)
            self.sent_e(u)
            self.sent_c(u)


class Inverse:
    def __init__(self, me, back, yi, xi, spec, rp, sq, rq, sr, rr, send, recv):
        self.me, self.back, self.yi, self.xi, self.spec = me, back, yi, xi, spec
        self.rp, self.sq, self.rq, self.sr, self.rr = rp, sq, rq, sr, rr
        self.send, self.recv = send, recv

    def sent_p(self, u):
        wait_for(self.rp.at[u, pl.ds(0, GX - 1)], self.send.at[0, u])

    def sent_q(self, u):
        wait_for(self.sq.at[u, pl.ds(0, HALF - 1)], self.send.at[1, u])

    def sent_r(self, u):
        wait_for(self.sr.at[u, pl.ds(0, HALF - 1)], self.send.at[3, u])

    def start(self, half, spec, unit, again):
        for c in range(CHUNKS):
            u = half * CHUNKS + c
            for kl in range(8):
                for pair in range(2):
                    unit[kl * 4 : kl * 4 + 4, pair * 128 : pair * 128 + 128] = spec[
                        c, kl, pair * 4 : pair * 4 + 4, :
                    ]
            if again:
                self.sent_p(u)
            self.spec[u] = unit[...].astype(BF)

        @pl.loop(half * CHUNKS, half * CHUNKS + CHUNKS)
        def _(u):
            column_spread(
                self.me, self.spec.at[u], self.rp.at[u], self.send.at[0, u], self.recv.at[0, u]
            )

    def stage_q(self, u, again):
        wait_for(self.rp.at[u], self.recv.at[0, u])
        if again:
            self.sent_q(u)
        block = self.rp[u].reshape(256, KZT)
        self.sq[u] = mm(self.xi[...], block).astype(BF).reshape(HALF, 16, KZT)
        half_exchange(
            self.me, self.sq.at[u], self.rq.at[u, self.me.hi],
            self.send.at[1, u], self.recv.at[1, u],
        )

    def stage_t(self, u):
        mine = self.rq.at[u, self.me.hi]
        wait_for(mine, self.recv.at[1, u])
        twin(self.me, mine, mine, self.send.at[2, u], self.recv.at[2, u])

    def stage_r(self, u, again):
        wait_for(self.rq.at[u, 1 - self.me.hi], self.recv.at[2, u])
        wait_for(self.sq.at[u], self.send.at[2, u])
        if again:
            self.sent_r(u)
        block = self.rq[u].reshape(256, KZT)
        self.sr[u] = mm(self.yi[...], block).astype(BF).reshape(HALF, 64, KZT)
        half_exchange(
            self.me, self.sr.at[u], self.rr.at[u], self.send.at[3, u], self.recv.at[3, u]
        )

    def ready(self, c):
        for half in range(2):
            u = half * CHUNKS + c
            wait_for(self.rr.at[u], self.recv.at[3, u])

    def branch(self, c, part, parts):
        count = XL // parts
        total = None
        for p in range(2):
            halves = []
            for half in range(2):
                block = self.rr[half * CHUNKS + c, pl.ds(part * (count // 2), count // 2)]
                block = block.astype(F32).reshape(count, 2, 2, YL, KZT)[:, :, p]
                block = [block[:, None, :, :, :128], block[:, None, :, :, 128:]]
                halves.append(jnp.concatenate(block, 1))
            lhs = jnp.concatenate(halves, -1).reshape(count * CR, KZT).astype(BF)
            term = mm(lhs, self.back[p * KZT : p * KZT + KZT, :])
            total = term if total is None else total + term
        return total

    def finish(self):
        @pl.loop(0, UNITS)
        def _(u):
            self.sent_p(u)
            self.sent_q(u)
            self.sent_r(u)


def run(schedule):
    steps = max(start + count for start, count, _ in schedule)

    @pl.loop(0, steps)
    def _(t):
        for start, count, stage in schedule:
            @pl.when(jnp.logical_and(t >= start, t < start + count))
            def _(stage=stage, start=start):
                stage(t - start)


TILES = 10
TILE = (TILES, 8, 128)


def swap_parts(tiles):
    even = (lax.rem(lax.broadcasted_iota(jnp.int32, TILE, 1), 2) == 0)
    return jnp.where(even, pltpu.roll(tiles, 7, 1), pltpu.roll(tiles, 1, 1)), even


def coefficient(modes, half, kl, i, part):
    row = pl.ds((i % CC) * 2 + part, 1)
    return jnp.broadcast_to(modes[half * CHUNKS + i // CC, kl, row, :], (8, 128))


def lay_out(modes, half, kl, flat):
    for c in range(CHUNKS):
        for part in range(2):
            flat[pl.ds(c * 16 + half * 2 + part, CC, 4), :] = modes[
                half * CHUNKS + c, kl, pl.ds(part, CC, 2), :
            ]


def mix_modes(modes, half, weight, flat, spec):
    @pl.loop(0, 8)
    def _(kl):
        by_real = jnp.zeros(TILE, F32)
        by_imag = jnp.zeros(TILE, F32)
        for i in range(C):
            block = weight[kl * C + i].astype(F32).reshape(TILE)
            by_real = by_real + block * coefficient(modes, half, kl, i, 0)[None]
            by_imag = by_imag + block * coefficient(modes, half, kl, i, 1)[None]
        turned, even = swap_parts(by_imag)
        mixed = by_real + jnp.where(even, -turned, turned)
        flat[...] = (mixed * mode_weight(TILE)).reshape(80, 128)
        for c in range(CHUNKS):
            for part in range(2):
                spec[c, kl, pl.ds(part, CC, 2), :] = flat[
                    pl.ds(c * 16 + half * 2 + part, CC, 4), :
                ]


def adjoint_modes(scaled, half, weight, flat, sums, spec):
    @pl.loop(0, 8)
    def _(kl):
        lay_out(scaled, half, kl, flat)
        grad = flat[...].reshape(TILE)
        turned, even = swap_parts(grad)
        turned = jnp.where(even, turned, -turned)
        for i in range(C):
            block = weight[kl * C + i].astype(F32).reshape(TILE)
            sums[0, i * 8 : i * 8 + 8] = (block * grad).sum(0)
            sums[1, i * 8 : i * 8 + 8] = (block * turned).sum(0)
        for c in range(CHUNKS):
            for part in range(2):
                total = None
                for row in (0, 1, 4, 5):
                    term = sums[part, pl.ds(c * 32 + half * 2 + row, CC, 8), :]
                    total = term if total is None else total + term
                spec[c, kl, pl.ds(part, CC, 2), :] = total


def gradient_kernel(modes, scaled, field, mixer, bias, out, field_out, mixer_out, bias_out, flat):
    field_out[...] = field[...]
    mixer_out[...] = mixer[...]
    bias_out[...] = bias[...]
    kl = pl.program_id(0)
    for half in range(2):
        lay_out(scaled, half, kl, flat)
    grad = flat[...].reshape(TILE)
    turned, even = swap_parts(grad)
    turned = jnp.where(even, turned, -turned)
    first = lax.rem(lax.broadcasted_iota(jnp.int32, (8, 128), 0), 4) < 2
    for i in range(C):
        real, imag = (
            jnp.where(first, coefficient(modes, 0, kl, i, p), coefficient(modes, 1, kl, i, p))
            for p in range(2)
        )
        out[i] = (grad * real[None] + turned * imag[None]).reshape(80, 128)


def channel_rows():
    rows = lax.broadcasted_iota(jnp.int32, (ROWS, C), 0)
    return lax.div(rows, YL) == lax.broadcasted_iota(jnp.int32, (ROWS, C), 1)


def same_place():
    rows = lax.broadcasted_iota(jnp.int32, (ROWS, ROWS), 0)
    columns = lax.broadcasted_iota(jnp.int32, (ROWS, ROWS), 1)
    return lax.rem(rows, YL) == lax.rem(columns, YL)


def spread_mixer(mixer, axis):
    spread = jnp.where(channel_rows(), 1.0, 0.0).astype(BF)
    half = lax.dot_general(
        spread, mixer, (((1,), (1 - axis,)), ((), ())), preferred_element_type=F32
    ).astype(BF)
    full = lax.dot_general(
        half, spread, (((1,), (1,)), ((), ())), preferred_element_type=F32
    )
    return jnp.where(same_place(), full, 0.0).astype(BF)


FORWARD_TABLES = [
    pltpu.VMEM((2, NZT, KZT), BF),
    pltpu.VMEM((256, 512), BF),
    pltpu.VMEM((256, 128), BF),
    pltpu.SemaphoreType.DMA((3,)),
]
INVERSE_TABLES = [
    pltpu.VMEM((2 * KZT, NZT), BF),
    pltpu.VMEM((512, 256), BF),
    pltpu.VMEM((128, 256), BF),
    pltpu.SemaphoreType.DMA((3,)),
]


def fetch_tables(me, depth_hbm, y_hbm, x_hbm, depth, y, x, sem):
    pairs = ((depth_hbm, depth), (y_hbm.at[me.hi], y), (x_hbm.at[me.gx], x))
    for n, (src, dst) in enumerate(pairs):
        local(src, dst, sem.at[n])

    def ready():
        for n, (_, dst) in enumerate(pairs):
            wait_for(dst, sem.at[n])

    return ready


def whole_kernel(
    x_hbm, cot_hbm, weight_hbm, mixer, bias, depth_hbm, yf_hbm, xf_hbm, back_hbm, yi_hbm, xi_hbm,
    out_hbm, modes, scaled, mixer_out, bias_out,
    gbuf, cbuf, point, weight, flat, sums, spec, unit, mixed, one, col, two, row,
    gsem, csem, wsem, small, *scratch
):
    me = Place()
    n = len(FORWARD_TABLES)
    depth, yf, xf, tsem, back, yi, xi, isem = scratch[: 2 * n]
    scratch = scratch[2 * n :]

    def chunk_of(ref, c):
        return ref.at[:, pl.ds(c * CR, CR), :]

    local(chunk_of(x_hbm, 0), gbuf.at[0], gsem.at[0])
    forward_ready = fetch_tables(me, depth_hbm, yf_hbm, xf_hbm, depth, yf, xf, tsem)

    @pl.loop(1, CHUNKS)
    def _(c):
        local(chunk_of(x_hbm, c), gbuf.at[c], gsem.at[c])

    local(weight_hbm, weight, wsem)
    inverse_ready = fetch_tables(me, back_hbm, yi_hbm, xi_hbm, back, yi, xi, isem)

    @pl.loop(0, CHUNKS)
    def _(c):
        local(chunk_of(cot_hbm, c), cbuf.at[c], csem.at[c])

    me.greet()
    n = len(INVERSE_SCRATCH)
    inv = Inverse(me, back, yi, xi, *scratch[:n])
    fwd = Forward(me, depth, yf, xf, *scratch[n:])
    flat[...] = jnp.zeros_like(flat)
    mixed[...] = jnp.zeros_like(mixed)
    forward_ready()

    def first_a(u):
        c = lax.rem(u, CHUNKS)

        @pl.when(u < CHUNKS)
        def _():
            wait_for(gbuf.at[c], gsem.at[c])

        table = depth[lax.div(u, CHUNKS)]
        for part in range(2):
            fwd.put(u, table, part, 2, gbuf[c, part * 8 : part * 8 + 8].reshape(8 * CR, NZT))
        fwd.send_a(u)

    def spectrum(half):
        if half == 0:
            wait_for(weight, wsem)
            inverse_ready()
        mix_modes(modes, half, weight, flat, spec)
        inv.start(half, spec, unit, False)

    def back_spectrum(half):
        adjoint_modes(scaled, half, weight, flat, sums, spec)
        inv.start(half, spec, unit, True)

    def pointwise(n):
        spread = spread_mixer(mixer[...], 0)
        shift = jnp.where(channel_rows(), bias[...], 0.0).sum(1, keepdims=True)
        for x in (2 * n, 2 * n + 1):
            point[x] = mm(spread, gbuf[:, x].reshape(ROWS, NZT)) + shift

    def slope(c):
        inv.ready(c)
        wait_for(cbuf.at[c], csem.at[c])
        fwd.sent_a(c)
        fwd.sent_a(CHUNKS + c)

        @pl.loop(0, 2)
        def _(part):
            rows = pl.ds(part * 8, 8)
            pre = inv.branch(c, part, 2)
            pre = pre + point[rows, pl.ds(c * CR, CR), :].reshape(8 * CR, NZT)
            cot = cbuf[c, rows].reshape(8 * CR, NZT).astype(F32)
            grad = (cot * gelu_slope(pre)).astype(BF)
            gbuf[c, rows] = grad.reshape(8, CR, NZT)
            for half in range(2):
                fwd.put(half * CHUNKS + c, depth[half], part, 2, grad)

        local(chunk_of(x_hbm, c), cbuf.at[c], csem.at[c])

    def pointwise_back(n):
        @pl.when(n == 0)
        def _():
            @pl.loop(0, CHUNKS)
            def _(c):
                wait_for(cbuf.at[c], csem.at[c])

        spread = spread_mixer(mixer[...], 1)
        contract = (((1,), (1,)), ((), ()))
        for x in (2 * n, 2 * n + 1):
            grad = gbuf[:, x].reshape(ROWS, NZT)
            point[x] = mm(spread, grad)
            mixed[:ROWS, :] += lax.dot_general(
                cbuf[:, x].reshape(ROWS, NZT), grad, contract, preferred_element_type=F32
            )
            mixed[ROWS:, :] += lax.dot_general(
                jnp.ones((8, NZT), BF), grad, contract, preferred_element_type=F32
            )

    def across_columns(_):
        kept = jnp.where(same_place(), mixed[:ROWS, :], 0.0).reshape(C, YL, ROWS).sum(1)
        stacked = jnp.concatenate([kept, mixed[ROWS : ROWS + 4, :]], 0)
        fold = lax.div(lax.broadcasted_iota(jnp.int32, (ROWS, 128), 0), YL)
        fold = fold == lax.broadcasted_iota(jnp.int32, (ROWS, 128), 1)
        one[...] = lax.dot_general(
            stacked, jnp.where(fold, 1.0, 0.0), (((1,), (0,)), ((), ())),
            precision=lax.Precision.HIGHEST, preferred_element_type=F32,
        )
        for d in range(1, GX):
            remote(one, col.at[me.gx], small.at[0], small.at[1], {"gx": me.x_peer(d)})
        local(one, col.at[me.gx], small.at[1])

    def across_rows(_):
        wait_for(col, small.at[1])
        total = col[0]
        for source in range(1, GX):
            total = total + col[source]
        two[...] = total
        for d in range(1, GY):
            remote(two, row.at[me.gy], small.at[2], small.at[3], {"gy": me.y_peer(d)})
        local(two, row.at[me.gy], small.at[3])

    def result(c):
        inv.ready(c)

        @pl.loop(0, 2)
        def _(part):
            rows = pl.ds(part * 8, 8)
            total = inv.branch(c, part, 2)
            total = total + point[rows, pl.ds(c * CR, CR), :].reshape(8 * CR, NZT)
            gbuf[c, rows] = total.astype(BF).reshape(8, CR, NZT)

        local(gbuf.at[c], chunk_of(out_hbm, c), gsem.at[c])

    send_b, send_e, send_c, send_d, send_q, send_t, send_r, send_s = SLACK
    at_b = send_b
    at_e = at_b + send_e
    at_c = at_e + send_c
    at_d = at_c + send_d
    at_p = at_d + CHUNKS - 1
    at_q = at_p + send_q
    at_t = at_q + send_t
    at_r = at_t + send_r
    at_s = at_r + CHUNKS + send_s
    run([
        (at_e, UNITS, lambda u: fwd.stage_e(u, False)),
        (at_s + at_e, UNITS, lambda u: fwd.stage_e(u, True)),
        (at_c, UNITS, lambda u: fwd.stage_c(u, False)),
        (at_s + at_c, UNITS, lambda u: fwd.stage_c(u, True)),
        (at_d, UNITS, lambda u: fwd.stage_d(u, modes, False)),
        (at_s + at_d, UNITS, lambda u: fwd.stage_d(u, scaled, True)),
        (at_q, UNITS, lambda u: inv.stage_q(u, False)),
        (at_s + at_q, UNITS, lambda u: inv.stage_q(u, True)),
        (at_t, UNITS, inv.stage_t),
        (at_s + at_t, UNITS, inv.stage_t),
        (at_b, UNITS, lambda u: fwd.stage_b(u, False)),
        (at_s + at_b, UNITS, lambda u: fwd.stage_b(u, True)),
        (at_r, UNITS, lambda u: inv.stage_r(u, False)),
        (at_s + at_r, UNITS, lambda u: inv.stage_r(u, True)),
        (0, UNITS, first_a),
        (at_s, CHUNKS, slope),
        (at_s, UNITS, fwd.send_a),
        (5, 8, pointwise),
        (at_p, 1, lambda _: spectrum(0)),
        (at_p + CHUNKS, 1, lambda _: spectrum(1)),
        (at_s + at_p, 1, lambda _: back_spectrum(0)),
        (at_s + at_p + CHUNKS, 1, lambda _: back_spectrum(1)),
        (at_s + 5, 8, pointwise_back),
        (at_s + 13, 1, across_columns),
        (at_s + 15, 1, across_rows),
        (at_s + at_s, CHUNKS, result),
    ])

    wait_for(row, small.at[3])
    total = row[0]
    for source in range(1, GY):
        total = total + row[source]
    total = total * (1.0 / math.sqrt(NX * NY * NZT))
    mixer_out[...] = total[:C, :C]
    bias_out[...] = total[C : C + 1, :C]
    wait_for(col.at[pl.ds(0, GX - 1)], small.at[0])
    wait_for(row.at[pl.ds(0, GY - 1)], small.at[2])

    @pl.loop(0, CHUNKS)
    def _(c):
        wait_for(gbuf.at[c], gsem.at[c])

    inv.finish()
    fwd.finish()


ANY = pl.BlockSpec(memory_space=pl.ANY)
VM = pl.BlockSpec(memory_space=pltpu.VMEM)


def params(number):
    return pltpu.CompilerParams(
        collective_id=number, has_side_effects=True, vmem_limit_bytes=60 * 2**20
    )


def body(layer_input, cotangent, spectral_weight, mixer_weight, bias_vector):
    depth, back, yf, yi, xf, xi = (jnp.asarray(v) for v in tables())
    grid = jnp.swapaxes(layer_input, 1, 2).reshape(XL, ROWS, NZT)
    cot = jnp.swapaxes(cotangent, 1, 2).reshape(XL, ROWS, NZT)
    weight = spectral_weight.reshape(8 * C, C, 2, 2, 128)
    weight = jnp.swapaxes(weight, 2, 3).reshape(8 * C, 4 * C, 128)
    modes_shape = jax.ShapeDtypeStruct((UNITS, 8, 8, 128), F32)
    chunked = pltpu.VMEM((CHUNKS, XL, CR, NZT), BF)
    chunk_sems = pltpu.SemaphoreType.DMA((CHUNKS,))
    flat = pltpu.VMEM((4 * C, 128), F32)

    input_grad, modes, scaled, mixer_grad, bias_grad = pl.pallas_call(
        whole_kernel,
        out_shape=[
            jax.ShapeDtypeStruct((XL, ROWS, NZT), BF),
            modes_shape,
            modes_shape,
            jax.ShapeDtypeStruct((C, C), F32),
            jax.ShapeDtypeStruct((1, C), F32),
        ],
        in_specs=[ANY, ANY, ANY, VM, VM] + [ANY] * 6,
        out_specs=[ANY, VM, VM, VM, VM],
        scratch_shapes=[
            chunked,
            chunked,
            pltpu.VMEM((XL, ROWS, NZT), F32),
            pltpu.VMEM((8 * C, 4 * C, 128), BF),
            flat,
            pltpu.VMEM((2, 8 * C, 128), F32),
            pltpu.VMEM((CHUNKS, 8, 8, 128), F32),
            pltpu.VMEM((32, KZT), F32),
            pltpu.VMEM((ROWS + 8, ROWS), F32),
            pltpu.VMEM((24, 128), F32),
            pltpu.VMEM((GX, 24, 128), F32),
            pltpu.VMEM((24, 128), F32),
            pltpu.VMEM((GY, 24, 128), F32),
            chunk_sems,
            chunk_sems,
            pltpu.SemaphoreType.DMA,
            pltpu.SemaphoreType.DMA((4,)),
        ]
        + FORWARD_TABLES
        + INVERSE_TABLES
        + INVERSE_SCRATCH
        + FORWARD_SCRATCH,
        compiler_params=params(1),
        name="whole",
    )(grid, cot, weight, mixer_weight, bias_vector.reshape(1, C), depth, yf, xf, back, yi, xi)

    field_spec = pl.BlockSpec((XL // 8, ROWS, NZT), lambda kl: (kl, 0, 0))
    modes_spec = pl.BlockSpec((UNITS, 8, 8, 128), lambda kl: (0, 0, 0, 0))
    spectral_grad, input_grad, mixer_grad, bias_grad = pl.pallas_call(
        gradient_kernel,
        out_shape=[
            jax.ShapeDtypeStruct((8 * C, 4 * C, 128), F32),
            jax.ShapeDtypeStruct((XL, ROWS, NZT), BF),
            jax.ShapeDtypeStruct((C, C), F32),
            jax.ShapeDtypeStruct((1, C), F32),
        ],
        grid=(8,),
        in_specs=[modes_spec, modes_spec, field_spec, VM, VM],
        out_specs=[pl.BlockSpec((C, 4 * C, 128), lambda kl: (kl, 0, 0)), field_spec, VM, VM],
        scratch_shapes=[flat],
        name="gradient",
    )(modes, scaled, input_grad, mixer_grad, bias_grad)
    spectral_grad = jnp.swapaxes(spectral_grad.reshape(8 * C, C, 2, 2, 128), 2, 3)
    spectral_grad = spectral_grad.reshape(4, 2, C, C, 2, KZT)
    input_grad = jnp.swapaxes(input_grad.reshape(XL, C, YL, NZT), 1, 2)
    return (input_grad, spectral_grad, mixer_grad, bias_grad.reshape(C))


def solution(mesh):
    return jax.shard_map(
        body,
        mesh=mesh,
        in_specs=(
            P("gx", "gy", None, None),
            P("gx", "gy", None, None),
            P("gx", "gy", None, None, None, None),
            P(),
            P(),
        ),
        out_specs=(P("gx", "gy", None, None), P("gx", "gy", None, None, None, None), P(), P()),
        check_vma=False,
    )
```
